128 devices in a mesh: gy: 8 (over z_lo, x), gx: 16 (over z_hi, y, core).
Axes of the slice: x: 4, y: 4, z: 4 (z_hi: 2, z_lo: 2; z = z_hi * 2 + z_lo), core: 2. Of those that a mesh axis runs over, the one named last changes fastest.
Arguments:
- tracers: float32 [2, 8, 2048, 4096], P(None, None, 'gy', 'gx'), may hold values from -8 to 12, as said below
- face_speeds: float32 [2, 2, 8, 2048, 4096], P(None, None, None, 'gy', 'gx'), may hold values from -0.25 to 0.25, as said below
- ocean_block: int32 [256, 32], P('gy', 'gx'), may hold values from 0 to 1, as said below
- ice_blocks: int32 [8192], P(('gy', 'gx')), may hold values from -1 to 8191, as said below
Outputs:
- new_tracers: float32 [2, 8, 2048, 4096], P(None, None, 'gy', 'gx')
- density: float32 [8, 2048, 4096], P(None, 'gy', 'gx')
- ice_surface: float32 [8192, 3, 8, 128], P(('gy', 'gx'))
The draws below stay inside these ranges and needn't reach their ends.
Inputs may be any that keep to these rules, and one draw needn't show every extreme that they name: `ocean_block`: 1 for an ocean block, 0 for land; at most half of the blocks of one device are land; some latitude block row has no land. `ice_blocks`: device d of the gy+gx order holds entries d * 64 to (d + 1) * 64 - 1, each the number of a block of its own latitude block row, or -1 for an empty slot. Every ocean block appears exactly once, no land block appears. At most 8 blocks of one device's grid go to one ice device, and this is reached in every draw; some ice device has all 64 slots filled in every draw. `tracers`: temperature anomalies lie within -8 to 12, salinity anomalies within -2 to 1.5. The top row's north faces are the fold: face_speeds[s, 1, k, 2047, i] = -face_speeds[s, 1, k, 2047, 4095 - i].
All inputs are finite; a program needn't handle non-finite values.
Results may differ from the reference program's by a relative error of at most 0.00002.
Values sent between devices are 32-bit elements; how exact they have to be, the bound alone decides.
A program may use at most 128 MiB of HBM per device.

```python
from functools import partial
import jax
import jax.numpy as jnp
from jax import lax

K = 8
CJ = 256
CI = 256
BJ = 8
BI = 128
STEPS = 2
NY = 2048
NX = 4096
TILE_ROWS = 256
TILE_COLS = 32
ICE_DEV = 64
CAP = 8
ICE_SLOTS = 8192
N_GY = 8
N_GX = 16


def one_order(sub_key):
    return jax.random.permutation(sub_key, ICE_DEV)


def ice_layout(key):
    land_key, rank_key, shift_key, sign_key, slot_key = jax.random.split(key, 5)
    per_device = ICE_DEV
    cols_device = CI // BI
    rows_device = CJ // BJ
    land_count = jax.random.randint(land_key, (N_GY, N_GX), 0, per_device // 2 + 1)
    land_count = land_count.at[0].set(0)
    rank_table = jax.vmap(one_order)(jax.random.split(rank_key, N_GY * N_GX)).reshape(N_GY, N_GX, per_device)
    is_ocean = (rank_table >= land_count[:, :, None]).astype(jnp.int32)
    ocean_rank = jnp.cumsum(is_ocean, axis=2) - is_ocean
    group_index = ocean_rank // CAP
    shifts = jax.random.randint(shift_key, (N_GY, 1, 1), 0, N_GX)
    turn_sign = 2 * jax.random.randint(sign_key, (N_GY, 1, 1), 0, 2) - 1
    column_ids = jnp.arange(N_GX, dtype=jnp.int32)[None, :, None]
    row_ids = jnp.arange(N_GY, dtype=jnp.int32)[:, None, None]
    target = (column_ids + shifts + turn_sign * group_index) % N_GX
    slot_orders = jax.vmap(one_order)(jax.random.split(slot_key, N_GY * N_GX)).reshape(N_GY, N_GX, per_device)
    slot_index = slot_orders[row_ids, target, jnp.minimum(ocean_rank, per_device - 1)]
    local_ids = jnp.arange(per_device, dtype=jnp.int32)[None, None, :]
    tile_ids = (row_ids * rows_device + local_ids // cols_device) * TILE_COLS + column_ids * cols_device + local_ids % cols_device
    position = jnp.where(is_ocean == 1, (row_ids * N_GX + target) * per_device + slot_index, ICE_SLOTS)
    block_list = jnp.full((ICE_SLOTS,), -1, jnp.int32).at[position.reshape(-1)].set(tile_ids.reshape(-1).astype(jnp.int32), mode='drop')
    land_grid = is_ocean.reshape(N_GY, N_GX, rows_device, cols_device).transpose(0, 2, 1, 3)
    return (land_grid.reshape(N_GY * rows_device, TILE_COLS), block_list)


def draw_ocean_block(key, part):
    layout = ice_layout(key)
    return layout[0]


def draw_ice_blocks(key, part):
    layout = ice_layout(key)
    return layout[1]


def draw_tracers(key, part):
    key = jax.random.fold_in(key, 3)
    raw_draw = jax.random.uniform(key, (2, K, NY, NX), jnp.float32)
    lower_end = jnp.array([-8.0, -2.0], jnp.float32)[:, None, None, None]
    spread = jnp.array([20.0, 3.5], jnp.float32)[:, None, None, None]
    return lower_end + spread * raw_draw


def draw_face_speeds(key, part):
    key = jax.random.fold_in(key, 5)
    raw_draw = jax.random.uniform(key, (STEPS, 2, K, NY, NX), jnp.float32, -1.0, 1.0)
    speeds = 0.25 * raw_draw
    top_row = speeds[:, 1, :, NY - 1, :]
    return speeds.at[:, 1, :, NY - 1, :].set(0.5 * (top_row - top_row[..., ::-1]))


def setup_inputs(seed: int = 0) -> dict:
    key_of = jax.random.split(jax.random.key(seed), 5)
    return {
        "tracers": draw_tracers(jax.random.fold_in(key_of[4], 71), 0),
        "face_speeds": draw_face_speeds(jax.random.fold_in(key_of[4], 71), 0),
        "ocean_block": draw_ocean_block(jax.random.fold_in(key_of[4], 71), 0),
        "ice_blocks": draw_ice_blocks(jax.random.fold_in(key_of[4], 71), 0),
    }


warming_swell_coefficient = 0.1655
haline_base = 0.7655
warming_swell_quadratic = 0.05952
haline_curve = 0.00054914
warming_compression_coupling = 0.0001497
haline_press = 0.00001109
mixing_contraction_coefficient = 0.0024341
lateral_mix = 0.08
mixing_base = 0.05
mixing_boost = 0.2


def seawater_mass_per_volume(heat_grid_values, saltiness_grid_values, depth_layer_count):
    return (-warming_swell_coefficient * (1.0 + 0.5 * warming_swell_quadratic * heat_grid_values + warming_compression_coupling * depth_layer_count) * heat_grid_values
            + haline_base * (1.0 - 0.5 * haline_curve * saltiness_grid_values - haline_press * depth_layer_count) * saltiness_grid_values
            - mixing_contraction_coefficient * heat_grid_values * saltiness_grid_values)


def face_flux(velocity, lower_cells, upper_cells):
    return jnp.maximum(velocity, 0.0) * lower_cells + jnp.minimum(velocity, 0.0) * upper_cells - lateral_mix * (upper_cells - lower_cells)


def level_update(ocean_mask, inputs):
    fields, east_speed, north_speed = inputs
    eastern = jnp.roll(fields, -1, axis=2)
    east_flux = face_flux(east_speed, fields, eastern)
    west_flux = jnp.roll(east_flux, 1, axis=2)
    northern = jnp.concatenate([fields[:, 1:], fields[:, -1:, ::-1]], axis=1)
    north_flux = face_flux(north_speed, fields, northern)
    south_flux = jnp.concatenate([jnp.zeros_like(north_flux[:, :1]), north_flux[:, :-1]], axis=1)
    return fields - ocean_mask * ((east_flux - west_flux) + (north_flux - south_flux))


def horizontal(fields, velocity, ocean_mask):
    stepped = lax.map(partial(level_update, ocean_mask), (jnp.moveaxis(fields, 1, 0), velocity[0], velocity[1]))
    return jnp.moveaxis(stepped, 0, 1)


def vertical(fields, density, ocean_mask):
    diffusivity = mixing_base + mixing_boost * jax.nn.sigmoid(-2.0 * (density[1:] - density[:-1]))
    vertical_flux = diffusivity * (fields[:, 1:] - fields[:, :-1])
    zero_layer = jnp.zeros_like(fields[:, :1])
    padded = jnp.concatenate([zero_layer, vertical_flux, zero_layer], axis=1)
    return fields + ocean_mask * (padded[:, 1:] - padded[:, :-1])


def reference(tracers, face_speeds, ocean_block, ice_blocks):
    ocean_mask = jnp.repeat(jnp.repeat(ocean_block.astype(jnp.float32), BJ, 0), BI, 1)
    depth_layer_count = (10.0 * jnp.arange(K, dtype=jnp.float32) + 5.0)[:, None, None]
    fields = tracers
    for step_index in range(STEPS):
        fields = horizontal(fields, face_speeds[step_index], ocean_mask)
        fields = vertical(fields, seawater_mass_per_volume(fields[0], fields[1], depth_layer_count), ocean_mask)
    density = seawater_mass_per_volume(fields[0], fields[1], depth_layer_count)
    surface = jnp.stack([fields[0, 0], fields[1, 0], density[0]])
    tile_stack = surface.reshape(3, TILE_ROWS, BJ, TILE_COLS, BI).transpose(1, 3, 0, 2, 4)
    tile_stack = tile_stack.reshape(TILE_ROWS * TILE_COLS, 3, BJ, BI)
    filled = ice_blocks >= 0
    picked = tile_stack[jnp.maximum(ice_blocks, 0)]
    ice_surface = jnp.where(filled[:, None, None, None], picked, 0.0)
    return fields, density, ice_surface
```

```python
import functools

import jax
import jax.numpy as jnp
from jax import lax
from jax.experimental import pallas as pl
from jax.experimental.pallas import tpu as pltpu
from jax.sharding import PartitionSpec as P

MESH = pl.DeviceIdType.MESH
LEVELS = 8
ROWS = 256
LANES = 128
STRIPS = 32
COLUMNS = 16
TOP = 7
CAP = 8
SLOTS = 64
FACES = 24
F32 = jnp.float32

warming_swell_coefficient = 0.1655
haline_base = 0.7655
warming_swell_quadratic = 0.05952
haline_curve = 0.00054914
warming_compression_coupling = 0.0001497
haline_press = 1.109e-05
mixing_contraction_coefficient = 0.0024341
lateral_mix = 0.08
mixing_base = 0.05
mixing_boost = 0.2


def density_at(heat, salt, level):
    depth = 10.0 * level + 5.0
    heat_one = -warming_swell_coefficient * (1.0 + warming_compression_coupling * depth)
    heat_two = -warming_swell_coefficient * 0.5 * warming_swell_quadratic
    salt_one = haline_base * (1.0 - haline_press * depth)
    salt_two = -haline_base * 0.5 * haline_curve
    return heat * (
        heat_one + heat_two * heat - mixing_contraction_coefficient * salt
    ) + salt * (salt_one + salt_two * salt)


def face_weights(speed):
    lower = jnp.maximum(speed, 0.0) + lateral_mix
    return lower, speed - lower


def face_flux(speed, lower_cells, upper_cells):
    lower, upper = face_weights(speed)
    return lower * lower_cells + upper * upper_cells


def sweep(x, speed, west, east, carry, mix, mask, first, last, resumed, dens, surf):
    lane = lax.broadcasted_iota(jnp.int32, (8, LANES), 1)
    sub = lax.broadcasted_iota(jnp.int32, (8, LANES), 0)
    first_lane, last_lane, first_row = lane == 0, lane == LANES - 1, sub == 0

    def advect(k, here, above, fw, fe, ocean):
        pu, qu, pv, qv = [], [], [], []
        for half in range(2):
            lower, upper = face_weights(speed[0, k, half, here, :])
            pu.append(lower)
            qu.append(upper)
            lower, upper = face_weights(speed[1, k, half, here, :])
            pv.append(lower)
            qv.append(upper)
        out = []
        for t in range(2):
            spot = t * LEVELS + k
            cells = [x[t, k, half, here, :] for half in range(2)]
            turned = [pltpu.roll(c, LANES - 1, 1) for c in cells]
            eastern = [jnp.where(last_lane, turned[1], turned[0]), turned[1]]
            ef = [pu[half] * cells[half] + qu[half] * eastern[half] for half in range(2)]
            ef[1] = jnp.where(last_lane, pltpu.roll(fe, LANES - 1 - spot, 1), ef[1])
            back = [pltpu.roll(f, 1, 1) for f in ef]
            edge = pltpu.roll(fw, LANES - spot, 1) if spot else fw
            wf = [jnp.where(first_lane, edge, back[0]), jnp.where(first_lane, back[0], back[1])]
            fields = []
            for half in range(2):
                nf = pv[half] * cells[half] + qv[half] * x[t, k, half, above, :]
                down = pltpu.roll(nf, 1, 0)
                sf = jnp.where(first_row, carry[t, k, half], down)
                carry[t, k, half] = down
                change = (ef[half] - wf[half]) + (nf - sf)
                fields.append(cells[half] - ocean[half] * change)
            out.append(fields)
        return out

    def strip(s, _):
        row = pl.multiple_of(s * 8, 8)
        here, above = pl.ds(row, 8), pl.ds(row + 1, 8)
        fw, fe = west[here, :], east[here, :]
        ocean = [mask[s, half].astype(F32) for half in range(2)]

        def settle(k, adv, flux, over):
            for half in range(2):
                done = []
                for t in range(2):
                    if flux is None:
                        gain = -over[t][half]
                    elif over is None:
                        gain = flux[t][half]
                    else:
                        gain = flux[t][half] - over[t][half]
                    value = adv[t][half] + ocean[half] * gain
                    x[t, k, half, here, :] = value
                    done.append(value)
                    if surf is not None and k == 0:
                        surf[2 * s + half, t] = value
                if dens is not None:
                    dens[k, half, here, :] = density_at(done[0], done[1], k)

        over = None
        if resumed:
            adv = [[x[t, first, half, here, :] for half in range(2)] for t in range(2)]
            over = [[mix[t, half, here, :] for half in range(2)] for t in range(2)]
        else:
            adv = advect(first, here, above, fw, fe, ocean)
        rho = [density_at(adv[0][half], adv[1][half], first) for half in range(2)]
        for k in range(first + 1, last + 1):
            lower = advect(k, here, above, fw, fe, ocean)
            rho_lower = [density_at(lower[0][half], lower[1][half], k) for half in range(2)]
            flux = [[None, None], [None, None]]
            for half in range(2):
                kappa = (mixing_base + 0.5 * mixing_boost) - 0.5 * mixing_boost * jnp.tanh(
                    rho_lower[half] - rho[half]
                )
                for t in range(2):
                    flux[t][half] = kappa * (lower[t][half] - adv[t][half])
            settle(k - 1, adv, flux, over)
            adv, rho, over = lower, rho_lower, flux
        if last == LEVELS - 1:
            settle(last, adv, None, over)
        else:
            for t in range(2):
                for half in range(2):
                    x[t, last, half, here, :] = adv[t][half]
                    mix[t, half, here, :] = over[t][half]
        return 0

    lax.fori_loop(0, STRIPS, strip, 0)


def pack(x, speed, e, levels, cols, rows):
    lane = lax.broadcasted_iota(jnp.int32, (8, LANES), 1)

    def group(g, _):
        to_east = jnp.zeros((8, LANES), F32)
        to_west = jnp.zeros((8, LANES), F32)
        for q in range(4):
            here = pl.ds(pl.multiple_of(g * 32 + q * 8, 8), 8)
            for k in levels:
                for t in range(2):
                    spot = 32 * q + t * LEVELS + k
                    value = pltpu.roll(x[t, k, 1, here, :], (spot + 1) % LANES, 1)
                    to_east = jnp.where(lane == spot, value, to_east)
                    value = x[t, k, 0, here, :]
                    if spot:
                        value = pltpu.roll(value, spot, 1)
                    to_west = jnp.where(lane == spot, value, to_west)
                for t in range(2):
                    spot = 32 * q + 16 + t * LEVELS + k
                    value = pltpu.roll(speed[0, k, 1, here, :], (spot + 1) % LANES, 1)
                    to_east = jnp.where(lane == spot, value, to_east)
        here = pl.ds(pl.multiple_of(g * 8, 8), 8)
        cols[e, 0, here, :] = to_east
        cols[e, 1, here, :] = to_west
        return 0

    lax.fori_loop(0, 8, group, 0)
    for k in levels:
        for half in range(2):
            for t in range(2):
                spot = t * 16 + k * 2 + half
                rows[e, 0, spot : spot + 1, :] = x[t, k, half, ROWS - 1 : ROWS, :]
                rows[e, 1, spot : spot + 1, :] = x[t, k, half, 0:1, :]
            spot = 32 + k * 2 + half
            rows[e, 0, spot : spot + 1, :] = speed[1, k, half, ROWS - 1 : ROWS, :]


def reversed_lanes(value):
    lane = lax.broadcasted_iota(jnp.int32, value.shape, 1)
    for bit in (1, 2, 4, 8, 16, 32, 64):
        upper = (lane & bit) != 0
        value = jnp.where(
            upper, pltpu.roll(value, bit, 1), pltpu.roll(value, LANES - bit, 1)
        )
    return value


def unpack(x, e, levels, cols, rows, cols_in, rows_in, west, east, carry, folded, top, open_south):
    def group(g, _):
        here = pl.ds(pl.multiple_of(g * 8, 8), 8)
        arrived, own = cols_in[e, 0, here, :], cols[e, 1, here, :]
        fw = face_flux(pltpu.roll(arrived, LANES - 16, 1), arrived, own)
        arrived, own = cols_in[e, 1, here, :], cols[e, 0, here, :]
        fe = face_flux(pltpu.roll(own, LANES - 16, 1), own, arrived)
        for q in range(4):
            here = pl.ds(pl.multiple_of(g * 32 + q * 8, 8), 8)
            west[here, :] = pltpu.roll(fw, LANES - 32 * q, 1) if q else fw
            east[here, :] = pltpu.roll(fe, LANES - 32 * q, 1) if q else fe
        return 0

    lax.fori_loop(0, 8, group, 0)
    speed = rows_in[e, 1, 32:48, :]
    for t in range(2):
        flux = face_flux(
            speed, rows_in[e, 1, 16 * t : 16 * t + 16, :], rows[e, 1, 16 * t : 16 * t + 16, :]
        )
        folded[16 * t : 16 * t + 16, :] = jnp.where(open_south, flux, 0.0)
    for k in levels:
        for half in range(2):
            for t in range(2):
                spot = t * 16 + k * 2 + half
                carry[t, k, half, 0:1, :] = folded[spot : spot + 1, :]

    @pl.when(top == 0)
    def _():
        folded[...] = rows_in[e, 0, 0:32, :]

    @pl.when(top == 1)
    def _():
        value = reversed_lanes(rows_in[e, 0, 0:32, :])
        odd = (lax.broadcasted_iota(jnp.int32, (32, LANES), 0) & 1) != 0
        folded[...] = jnp.where(odd, pltpu.roll(value, 1, 0), pltpu.roll(value, 31, 0))

    for k in levels:
        for half in range(2):
            for t in range(2):
                spot = t * 16 + k * 2 + half
                x[t, k, half, ROWS : ROWS + 1, :] = folded[spot : spot + 1, :]


def running_count(flags):
    lane = lax.broadcasted_iota(jnp.int32, flags.shape, 1)
    total = flags
    for shift in (1, 2, 4, 8, 16, 32):
        total = total + jnp.where(lane >= shift, pltpu.roll(total, shift, 1), 0)
    return total - flags


def lane_total(value):
    for shift in (1, 2, 4, 8, 16, 32, 64):
        value = value + pltpu.roll(value, shift, 1)
    return value


def send_table(lists, gx, stage, table):
    for p in range(COLUMNS):
        stage[p : p + 1, :] = lists[p, 0:1, :]
    ids = stage[...]
    lane = lax.broadcasted_iota(jnp.int32, ids.shape, 1)
    mine = ((ids & 31) >> 1 == gx) & (ids >= 0)
    rank = running_count(jnp.where(mine, 1, 0))
    tile = ((ids >> 5) & (STRIPS - 1)) * 2 + (ids & 1)
    out = jnp.zeros_like(ids)
    for r in range(CAP):
        found = lane_total(jnp.where(mine & (rank == r), tile, 0))
        out = jnp.where(lane == r, found, out)
    table[...] = out


def pick_table(lists, gx, out):
    ids = jnp.broadcast_to(lists[gx, 0:1, :], (COLUMNS, LANES))
    row = lax.broadcasted_iota(jnp.int32, ids.shape, 0)
    mine = ((ids & 31) >> 1 == row) & (ids >= 0)
    flags = jnp.where(mine, 1, 0)
    place = jnp.where(mine, running_count(flags) + row * CAP + 1, 0)
    both = place[0:8] + place[8:16]
    for shift in (4, 2, 1):
        both = both + pltpu.roll(both, shift, 0)
    out[...] = both - 1


def ocean_kernel(
    tracers, speeds, mask, own_list, x, dens, incoming, picks,
    speed, cols, rows, cols_in, rows_in, west, east, carry, mix, folded,
    lists, stage, table, table_s, surf, outgoing,
    load_sem, send_sem, recv_sem, list_send, list_recv, relay_send, relay_recv, local_sem,
):
    gy, gx = lax.axis_index("gy"), lax.axis_index("gx")
    top = gy // TOP
    inner = (gy + TOP - 1) // TOP
    east_at = lax.rem(gx + 1, COLUMNS)
    west_at = lax.rem(gx + COLUMNS - 1, COLUMNS)
    north_row = gy + 1 - top
    north_col = gx + top * (COLUMNS - 1 - 2 * gx)

    barrier = pltpu.get_barrier_semaphore()

    def greet(d, _):
        peer = lax.rem(gx + 1 + d, COLUMNS)
        pl.semaphore_signal(barrier, inc=1, device_id=(gy, peer), device_id_type=MESH)
        return 0

    lax.fori_loop(0, COLUMNS - 1, greet, 0)

    @pl.when(gy < TOP)
    def _():
        pl.semaphore_signal(barrier, inc=1, device_id=(gy + 1, gx), device_id_type=MESH)

    @pl.when(gy > 0)
    def _():
        pl.semaphore_signal(barrier, inc=1, device_id=(gy - 1, gx), device_id_type=MESH)

    def load_x(i, lo, hi):
        return [
            pltpu.make_async_copy(
                tracers.at[:, pl.ds(lo, hi - lo), :, pl.ds(half * LANES, LANES)],
                x.at[:, pl.ds(lo, hi - lo), half, pl.ds(0, ROWS), :],
                load_sem.at[i, half],
            )
            for half in range(2)
        ]

    def load_speed(i, step, lo, hi):
        return [
            pltpu.make_async_copy(
                speeds.at[step, :, pl.ds(lo, hi - lo), :, pl.ds(half * LANES, LANES)],
                speed.at[step, :, pl.ds(lo, hi - lo), half],
                load_sem.at[i, half],
            )
            for half in range(2)
        ]

    early = load_x(0, 0, 3) + load_speed(1, 0, 0, 3) + load_x(2, 3, 8) + load_speed(3, 0, 3, 8)
    late_low = load_speed(4, 1, 0, 2)
    late_high = load_speed(5, 1, 2, 8)
    for c in early + late_low + late_high:
        c.start()

    lists[gx] = jnp.full((8, LANES), -1, jnp.int32)
    lists[gx, :, 0:SLOTS] = jnp.broadcast_to(own_list[...], (8, SLOTS))

    for c in early:
        c.wait()
    pack(x, speed.at[0], 0, range(LEVELS), cols, rows)

    pl.semaphore_wait(barrier, COLUMNS - 1 + (1 - top) + inner)

    def send_edges(e):
        return [
            pltpu.make_async_remote_copy(
                cols.at[e, 0], cols_in.at[e, 0], send_sem.at[e, 0], recv_sem.at[e, 0],
                device_id=(gy, east_at), device_id_type=MESH,
            ),
            pltpu.make_async_remote_copy(
                cols.at[e, 1], cols_in.at[e, 1], send_sem.at[e, 1], recv_sem.at[e, 1],
                device_id=(gy, west_at), device_id_type=MESH,
            ),
            pltpu.make_async_remote_copy(
                rows.at[e, 0], rows_in.at[e, 1 - top], send_sem.at[e, 2], recv_sem.at[e, 3 - top],
                device_id=(north_row, north_col), device_id_type=MESH,
            ),
        ]

    def send_south(e):
        return pltpu.make_async_remote_copy(
            rows.at[e, 1], rows_in.at[e, 0], send_sem.at[e, 3], recv_sem.at[e, 2],
            device_id=(gy - 1, gx), device_id_type=MESH,
        )

    def start_edges(e):
        for c in send_edges(e):
            c.start()

        @pl.when(gy > 0)
        def _():
            send_south(e).start()

    def wait_edges(e):
        to_east, to_west, to_north = send_edges(e)
        to_east.wait_recv()
        to_west.wait_recv()
        pltpu.make_async_remote_copy(
            rows.at[e, 0], rows_in.at[e, 0], send_sem.at[e, 2], recv_sem.at[e, 2],
            device_id=(north_row, north_col), device_id_type=MESH,
        ).wait_recv()

        @pl.when(gy > 0)
        def _():
            pltpu.make_async_remote_copy(
                rows.at[e, 0], rows_in.at[e, 1], send_sem.at[e, 2], recv_sem.at[e, 3],
                device_id=(north_row, north_col), device_id_type=MESH,
            ).wait_recv()

    def finish_edges(e):
        for c in send_edges(e):
            c.wait_send()

        @pl.when(gy > 0)
        def _():
            send_south(e).wait_send()

    start_edges(0)

    def list_copy(peer, slot):
        return pltpu.make_async_remote_copy(
            lists.at[gx], lists.at[slot], list_send.at[peer], list_recv.at[slot],
            device_id=(gy, peer), device_id_type=MESH,
        )

    def send_list(d, _):
        list_copy(lax.rem(gx + 1 + d, COLUMNS), gx).start()
        return 0

    lax.fori_loop(0, COLUMNS - 1, send_list, 0)

    def fill(e, levels):
        wait_edges(e)
        unpack(x, e, levels, cols, rows, cols_in, rows_in, west, east, carry, folded, top, gy > 0)

    fill(0, range(LEVELS))
    sweep(x, speed.at[0], west, east, carry, mix, mask, 0, 2, False, None, None)
    for c in late_low:
        c.wait()
    pack(x, speed.at[1], 1, range(0, 2), cols, rows)
    start_edges(1)
    sweep(x, speed.at[0], west, east, carry, mix, mask, 2, 7, True, None, None)
    for c in late_high:
        c.wait()
    pack(x, speed.at[1], 2, range(2, 8), cols, rows)
    start_edges(2)

    def take_list(d, _):
        peer = lax.rem(gx + 1 + d, COLUMNS)
        list_copy(peer, peer).wait_recv()
        return 0

    lax.fori_loop(0, COLUMNS - 1, take_list, 0)
    send_table(lists, gx, stage, table)
    fetch = pltpu.make_async_copy(table, table_s, local_sem)
    fetch.start()
    pick_table(lists, gx, picks)

    fill(1, range(0, 2))
    sweep(x, speed.at[1], west, east, carry, mix, mask, 0, 1, False, dens, surf)
    fetch.wait()

    def bucket(peer, target, base):
        def slot(r, _):
            tile = jnp.clip(table_s[peer, r], 0, SLOTS - 1)
            target[base + r] = surf[tile]
            return 0

        lax.fori_loop(0, CAP, slot, 0)

    def relay_copy(peer, slot):
        return pltpu.make_async_remote_copy(
            outgoing.at[pl.ds(peer * CAP, CAP)], incoming.at[pl.ds(slot * CAP, CAP)],
            relay_send.at[peer], relay_recv.at[slot],
            device_id=(gy, peer), device_id_type=MESH,
        )

    def relay(d, _):
        peer = lax.rem(gx + 1 + lax.rem(d + 7, COLUMNS - 1), COLUMNS)
        bucket(peer, outgoing, peer * CAP)
        relay_copy(peer, gx).start()
        return 0

    lax.fori_loop(0, COLUMNS - 1, relay, 0)
    bucket(gx, incoming, gx * CAP)

    fill(2, range(2, 8))
    sweep(x, speed.at[1], west, east, carry, mix, mask, 1, 7, True, dens, None)

    for e in range(3):
        finish_edges(e)

    def close(d, _):
        peer = lax.rem(gx + 1 + d, COLUMNS)
        list_copy(peer, gx).wait_send()
        relay_copy(peer, gx).wait_send()
        relay_copy(peer, peer).wait_recv()
        return 0

    lax.fori_loop(0, COLUMNS - 1, close, 0)


def output_kernel(x, dens, incoming, picks, tracers_out, dens_out, ice_out, ice, sems):
    copies = []
    for half in range(2):
        lanes = pl.ds(half * LANES, LANES)
        copies.append(
            pltpu.make_async_copy(
                x.at[:, :, half, pl.ds(0, ROWS), :], tracers_out.at[:, :, :, lanes], sems.at[half]
            )
        )
        copies.append(
            pltpu.make_async_copy(
                dens.at[:, half], dens_out.at[:, :, lanes], sems.at[2 + half]
            )
        )
    for c in copies:
        c.start()

    def slot(s, _):
        place = picks[0, s]
        filled = place >= 0
        spot = jnp.clip(place, 0, COLUMNS * CAP - 1)
        heat = jnp.where(filled, incoming[spot, 0], 0.0)
        salt = jnp.where(filled, incoming[spot, 1], 0.0)
        ice[s, 0] = heat
        ice[s, 1] = salt
        ice[s, 2] = density_at(heat, salt, 0)
        return 0

    for part in range(2):
        lax.fori_loop(part * 32, part * 32 + 32, slot, 0)
        c = pltpu.make_async_copy(
            ice.at[pl.ds(part * 32, 32)], ice_out.at[pl.ds(part * 32, 32)], sems.at[4 + part]
        )
        c.start()
        copies.append(c)
    for c in copies:
        c.wait()


def on_device(tracers, face_speeds, ocean_block, ice_blocks):
    anywhere = pl.BlockSpec(memory_space=pl.ANY)
    vmem = pl.BlockSpec(memory_space=pltpu.VMEM)
    smem = pl.BlockSpec(memory_space=pltpu.SMEM)
    dma = pltpu.SemaphoreType.DMA
    x, dens, incoming, picks = pl.pallas_call(
        ocean_kernel,
        out_shape=(
            jax.ShapeDtypeStruct((2, LEVELS, 2, ROWS + 8, LANES), F32),
            jax.ShapeDtypeStruct((LEVELS, 2, ROWS, LANES), F32),
            jax.ShapeDtypeStruct((COLUMNS * CAP, 2, 8, LANES), F32),
            jax.ShapeDtypeStruct((8, LANES), jnp.int32),
        ),
        in_specs=[anywhere, anywhere, smem, vmem],
        out_specs=(vmem, vmem, vmem, vmem),
        scratch_shapes=[
            pltpu.VMEM((2, 2, LEVELS, 2, ROWS, LANES), F32),
            pltpu.VMEM((3, 2, 64, LANES), F32),
            pltpu.VMEM((3, 2, 48, LANES), F32),
            pltpu.VMEM((3, 2, 64, LANES), F32),
            pltpu.VMEM((3, 2, 48, LANES), F32),
            pltpu.VMEM((ROWS, LANES), F32),
            pltpu.VMEM((ROWS, LANES), F32),
            pltpu.VMEM((2, LEVELS, 2, 8, LANES), F32),
            pltpu.VMEM((2, 2, ROWS, LANES), F32),
            pltpu.VMEM((32, LANES), F32),
            pltpu.VMEM((COLUMNS, 8, LANES), jnp.int32),
            pltpu.VMEM((COLUMNS, LANES), jnp.int32),
            pltpu.VMEM((COLUMNS, LANES), jnp.int32),
            pltpu.SMEM((COLUMNS, LANES), jnp.int32),
            pltpu.VMEM((SLOTS, 2, 8, LANES), F32),
            pltpu.VMEM((COLUMNS * CAP, 2, 8, LANES), F32),
            dma((6, 2)),
            dma((3, 4)),
            dma((3, 4)),
            dma((COLUMNS,)),
            dma((COLUMNS,)),
            dma((COLUMNS,)),
            dma((COLUMNS,)),
            dma,
        ],
        compiler_params=pltpu.CompilerParams(
            collective_id=0, has_side_effects=True, vmem_limit_bytes=48 << 20
        ),
        name="ocean",
    )(tracers, face_speeds, ocean_block, ice_blocks.reshape(1, SLOTS))
    return pl.pallas_call(
        output_kernel,
        out_shape=(
            jax.ShapeDtypeStruct(tracers.shape, F32),
            jax.ShapeDtypeStruct(tracers.shape[1:], F32),
            jax.ShapeDtypeStruct((SLOTS, 3, 8, LANES), F32),
        ),
        in_specs=[anywhere, anywhere, vmem, smem],
        out_specs=(anywhere, anywhere, anywhere),
        scratch_shapes=[pltpu.VMEM((SLOTS, 3, 8, LANES), F32), dma((6,))],
        compiler_params=pltpu.CompilerParams(vmem_limit_bytes=16 << 20),
        name="outputs",
    )(x, dens, incoming, picks)


def solution(mesh):
    return jax.shard_map(
        on_device,
        mesh=mesh,
        in_specs=(
            P(None, None, "gy", "gx"),
            P(None, None, None, "gy", "gx"),
            P("gy", "gx"),
            P(("gy", "gx")),
        ),
        out_specs=(
            P(None, None, "gy", "gx"),
            P(None, "gy", "gx"),
            P(("gy", "gx"), None, None, None),
        ),
        check_vma=False,
    )
```

```python
import functools

import jax
import jax.numpy as jnp
from jax import lax
from jax.experimental import pallas as pl
from jax.experimental.pallas import tpu as pltpu
from jax.sharding import PartitionSpec as P

MESH = pl.DeviceIdType.MESH
LEVELS = 8
ROWS = 256
LANES = 128
STRIPS = 32
CHUNK = 64
COLUMNS = 16
TOP = 7
CAP = 8
SLOTS = 64
FACES = 24
F32 = jnp.float32

warming_swell_coefficient = 0.1655
haline_base = 0.7655
warming_swell_quadratic = 0.05952
haline_curve = 0.00054914
warming_compression_coupling = 0.0001497
haline_press = 1.109e-05
mixing_contraction_coefficient = 0.0024341
lateral_mix = 0.08
mixing_base = 0.05
mixing_boost = 0.2


def density_at(heat, salt, level):
    depth = 10.0 * level + 5.0
    heat_one = -warming_swell_coefficient * (1.0 + warming_compression_coupling * depth)
    heat_two = -warming_swell_coefficient * 0.5 * warming_swell_quadratic
    salt_one = haline_base * (1.0 - haline_press * depth)
    salt_two = -haline_base * 0.5 * haline_curve
    return heat * (
        heat_one + heat_two * heat - mixing_contraction_coefficient * salt
    ) + salt * (salt_one + salt_two * salt)


def face_weights(speed):
    lower = jnp.maximum(speed, 0.0) + lateral_mix
    return lower, speed - lower


def face_flux(speed, lower_cells, upper_cells):
    lower, upper = face_weights(speed)
    return lower * lower_cells + upper * upper_cells


def advance(x, speed, ocean_v, low, high):
    lane = lax.broadcasted_iota(jnp.int32, (ROWS, LANES), 1)
    first_lane, last_lane = lane == 0, lane == LANES - 1
    last_row = lax.broadcasted_iota(jnp.int32, (8, LANES), 0) == 7
    here, above = pl.ds(0, ROWS), pl.ds(1, ROWS)

    def level(k, _):
        east = [face_weights(speed[0, k, half]) for half in range(2)]
        north = [face_weights(speed[1, k, half]) for half in range(2)]
        for t in range(2):
            cells = [x[t, k, half, here, :] for half in range(2)]
            turned = [pltpu.roll(c, LANES - 1, 1) for c in cells]
            eastern = [jnp.where(last_lane, turned[1], turned[0]), turned[1]]
            ef = [east[half][0] * cells[half] + east[half][1] * eastern[half] for half in range(2)]
            ef[1] = jnp.where(last_lane, 0.0, ef[1])
            back = [pltpu.roll(f, 1, 1) for f in ef]
            wf = [jnp.where(first_lane, 0.0, back[0]), jnp.where(first_lane, back[0], back[1])]
            for half in range(2):
                nf = north[half][0] * cells[half] + north[half][1] * x[t, k, half, above, :]
                nf = jnp.concatenate(
                    [nf[: ROWS - 8], jnp.where(last_row, 0.0, nf[ROWS - 8 :])], axis=0
                )
                change = (ef[half] - wf[half]) + (nf - pltpu.roll(nf, 1, 0))
                x[t, k, half, here, :] = cells[half] - ocean_v[half] * change
        return 0

    lax.fori_loop(low, high, level, 0)


def settle_levels(x, edge, mix, ocean_v, first, last, resumed, dens, surf):
    lane = lax.broadcasted_iota(jnp.int32, (CHUNK, LANES), 1)
    first_lane, last_lane = lane == 0, lane == LANES - 1

    def chunk(c, _):
        here = pl.ds(pl.multiple_of(c * CHUNK, CHUNK), CHUNK)
        rim = edge[here, :]
        ocean = [ocean_v[half, here, :] for half in range(2)]

        def advected(k):
            out = []
            for t in range(2):
                ends = pltpu.roll(rim, LANES - 1 - 2 * (t * LEVELS + k), 1)
                out.append(
                    [
                        x[t, k, 0, here, :] + jnp.where(first_lane, ends, 0.0),
                        x[t, k, 1, here, :] + jnp.where(last_lane, ends, 0.0),
                    ]
                )
            return out

        def settle(k, adv, flux, over):
            for half in range(2):
                done = []
                for t in range(2):
                    if flux is None:
                        gain = -over[t][half]
                    elif over is None:
                        gain = flux[t][half]
                    else:
                        gain = flux[t][half] - over[t][half]
                    value = adv[t][half] + ocean[half] * gain
                    x[t, k, half, here, :] = value
                    done.append(value)
                    if surf is not None and k == 0:
                        for i in range(CHUNK // 8):
                            tile = 2 * (c * (CHUNK // 8) + i) + half
                            surf[tile, t] = value[8 * i : 8 * i + 8]
                if dens is not None:
                    dens[k, half, here, :] = density_at(done[0], done[1], k)

        over = None
        if resumed:
            adv = [[x[t, first, half, here, :] for half in range(2)] for t in range(2)]
            over = [[mix[t, half, here, :] for half in range(2)] for t in range(2)]
        else:
            adv = advected(first)
        rho = [density_at(adv[0][half], adv[1][half], first) for half in range(2)]
        for k in range(first + 1, last + 1):
            lower = advected(k)
            rho_lower = [density_at(lower[0][half], lower[1][half], k) for half in range(2)]
            flux = [[None, None], [None, None]]
            for half in range(2):
                kappa = (mixing_base + 0.5 * mixing_boost) - 0.5 * mixing_boost * jnp.tanh(
                    rho_lower[half] - rho[half]
                )
                for t in range(2):
                    flux[t][half] = kappa * (lower[t][half] - adv[t][half])
            settle(k - 1, adv, flux, over)
            adv, rho, over = lower, rho_lower, flux
        if last == LEVELS - 1:
            settle(last, adv, None, over)
        else:
            for t in range(2):
                for half in range(2):
                    x[t, last, half, here, :] = adv[t][half]
                    mix[t, half, here, :] = over[t][half]
        return 0

    lax.fori_loop(0, ROWS // CHUNK, chunk, 0)


def aligned(index):
    return index if isinstance(index, int) else pl.multiple_of(index, 8)


def pack(x, speed, e, levels, cols, rows):
    lane = lax.broadcasted_iota(jnp.int32, (8, LANES), 1)

    def group(g, _):
        parts = []
        for q in range(4):
            here = pl.ds(aligned(g * 32 + q * 8), 8)
            east = jnp.zeros((8, LANES), F32)
            west = jnp.zeros((8, LANES), F32)
            face = jnp.zeros((8, LANES), F32)
            for k in levels:
                for t in range(2):
                    spot = 32 * q + 2 * (t * LEVELS + k)
                    value = pltpu.roll(x[t, k, 1, here, :], spot + 1, 1)
                    east = jnp.where(lane == spot, value, east)
                    value = pltpu.roll(x[t, k, 0, here, :], spot + 1, 1)
                    west = jnp.where(lane == spot + 1, value, west)
                spot = 32 * q + 2 * k + 1
                value = pltpu.roll(speed[0, k, 1, here, :], spot + 1, 1)
                face = jnp.where(lane == spot, value, face)
            parts.append((east, west, face))
        east, west, face = [
            (parts[0][i] + parts[1][i]) + (parts[2][i] + parts[3][i]) for i in range(3)
        ]
        here = pl.ds(aligned(g * 8), 8)
        cols[e, 0, here, :] = (east + face) + pltpu.roll(face, 2 * LEVELS, 1)
        cols[e, 1, here, :] = west
        return 0

    if len(levels) <= 3:
        for g in range(8):
            group(g, 0)
    else:
        lax.fori_loop(0, 8, group, 0, unroll=2)
    for k in levels:
        for half in range(2):
            for t in range(2):
                spot = t * 16 + k * 2 + half
                rows[e, 0, spot : spot + 1, :] = x[t, k, half, ROWS - 1 : ROWS, :]
                rows[e, 1, spot : spot + 1, :] = x[t, k, half, 0:1, :]
            spot = 32 + k * 2 + half
            rows[e, 0, spot : spot + 1, :] = speed[1, k, half, ROWS - 1 : ROWS, :]


def reversed_lanes(value):
    lane = lax.broadcasted_iota(jnp.int32, value.shape, 1)
    for bit in (1, 2, 4, 8, 16, 32, 64):
        upper = (lane & bit) != 0
        value = jnp.where(
            upper, pltpu.roll(value, bit, 1), pltpu.roll(value, LANES - bit, 1)
        )
    return value


def unpack(x, e, levels, cols, rows, cols_in, rows_in, edge, ocean_v, flows, top, open_south):
    odd = (lax.broadcasted_iota(jnp.int32, (8, LANES), 1) & 1) != 0
    for g in range(8):
        here = pl.ds(g * 8, 8)
        arrived = cols_in[e, 0, here, :]
        fw = face_flux(arrived, pltpu.roll(arrived, 1, 1), cols[e, 1, here, :])
        own, arrived = cols[e, 0, here, :], cols_in[e, 1, here, :]
        fe = face_flux(pltpu.roll(own, LANES - 1, 1), own, pltpu.roll(arrived, LANES - 1, 1))
        both = jnp.where(odd, fw, -fe)
        for q in range(4):
            here = pl.ds(g * 32 + q * 8, 8)
            ocean = jnp.where(odd, ocean_v[0, here, :], ocean_v[1, here, :])
            edge[e, here, :] = (pltpu.roll(both, LANES - 32 * q, 1) if q else both) * ocean

    right = (lax.broadcasted_iota(jnp.int32, (16, LANES), 0) & 1) != 0
    low = jnp.where(right, ocean_v[1, 0:1, :], ocean_v[0, 0:1, :])
    high = jnp.where(right, ocean_v[1, ROWS - 1 : ROWS, :], ocean_v[0, ROWS - 1 : ROWS, :])
    speed = rows_in[e, 1, 32:48, :]
    for t in range(2):
        part = pl.ds(16 * t, 16)
        flux = face_flux(speed, rows_in[e, 1, part, :], rows[e, 1, part, :])
        flows[0, part, :] = jnp.where(open_south, low * flux, 0.0)

    def north(arrived):
        for t in range(2):
            part = pl.ds(16 * t, 16)
            flux = face_flux(rows[e, 0, 32:48, :], rows[e, 0, part, :], arrived[16 * t : 16 * t + 16])
            flows[1, part, :] = -high * flux

    @pl.when(top == 0)
    def _():
        north(rows_in[e, 0, 0:32, :])

    @pl.when(top == 1)
    def _():
        value = reversed_lanes(rows_in[e, 0, 0:32, :])
        odd_row = (lax.broadcasted_iota(jnp.int32, (32, LANES), 0) & 1) != 0
        north(jnp.where(odd_row, pltpu.roll(value, 1, 0), pltpu.roll(value, 31, 0)))

    for k in levels:
        for half in range(2):
            for t in range(2):
                spot = t * 16 + k * 2 + half
                x[t, k, half, 0:1, :] += flows[0, spot : spot + 1, :]
                x[t, k, half, ROWS - 1 : ROWS, :] += flows[1, spot : spot + 1, :]


def running_count(flags):
    lane = lax.broadcasted_iota(jnp.int32, flags.shape, 1)
    total = flags
    for shift in (1, 2, 4, 8, 16, 32):
        total = total + jnp.where(lane >= shift, pltpu.roll(total, shift, 1), 0)
    return total - flags


def lane_total(value):
    for shift in (1, 2, 4, 8, 16, 32, 64):
        value = value + pltpu.roll(value, shift, 1)
    return value


def send_table(lists, gx, stage, table):
    for p in range(COLUMNS):
        stage[p : p + 1, :] = lists[p, 0:1, :]
    ids = stage[...]
    lane = lax.broadcasted_iota(jnp.int32, ids.shape, 1)
    mine = ((ids & 31) >> 1 == gx) & (ids >= 0)
    rank = running_count(jnp.where(mine, 1, 0))
    tile = ((ids >> 5) & (STRIPS - 1)) * 2 + (ids & 1)
    out = jnp.zeros_like(ids)
    for r in range(CAP):
        found = lane_total(jnp.where(mine & (rank == r), tile, 0))
        out = jnp.where(lane == r, found, out)
    table[...] = out


def pick_table(lists, gx, out):
    ids = jnp.broadcast_to(lists[gx, 0:1, :], (COLUMNS, LANES))
    row = lax.broadcasted_iota(jnp.int32, ids.shape, 0)
    mine = ((ids & 31) >> 1 == row) & (ids >= 0)
    flags = jnp.where(mine, 1, 0)
    place = jnp.where(mine, running_count(flags) + row * CAP + 1, 0)
    both = place[0:8] + place[8:16]
    for shift in (4, 2, 1):
        both = both + pltpu.roll(both, shift, 0)
    out[...] = both - 1


def ocean_kernel(
    tracers, speeds, land, own_list, x, dens, incoming, picks,
    speed, cols, rows, cols_in, rows_in, edge, mix, ocean_v, flows, own_v, mask,
    lists, stage, table, table_s, surf, outgoing,
    load_sem, send_sem, recv_sem, list_send, list_recv, relay_send, relay_recv, local_sem,
):
    gy, gx = lax.axis_index("gy"), lax.axis_index("gx")
    top = gy // TOP
    inner = (gy + TOP - 1) // TOP
    east_at = lax.rem(gx + 1, COLUMNS)
    west_at = lax.rem(gx + COLUMNS - 1, COLUMNS)
    north_row = gy + 1 - top
    north_col = gx + top * (COLUMNS - 1 - 2 * gx)

    barrier = pltpu.get_barrier_semaphore()

    def greet(d, _):
        peer = lax.rem(gx + 1 + d, COLUMNS)
        pl.semaphore_signal(barrier, inc=1, device_id=(gy, peer), device_id_type=MESH)
        return 0

    lax.fori_loop(0, COLUMNS - 1, greet, 0)

    @pl.when(gy < TOP)
    def _():
        pl.semaphore_signal(barrier, inc=1, device_id=(gy + 1, gx), device_id_type=MESH)

    @pl.when(gy > 0)
    def _():
        pl.semaphore_signal(barrier, inc=1, device_id=(gy - 1, gx), device_id_type=MESH)

    def load_x(i, lo, hi):
        return [
            pltpu.make_async_copy(
                tracers.at[:, pl.ds(lo, hi - lo), :, pl.ds(half * LANES, LANES)],
                x.at[:, pl.ds(lo, hi - lo), half, pl.ds(0, ROWS), :],
                load_sem.at[i, half],
            )
            for half in range(2)
        ]

    def load_speed(i, step, lo, hi):
        return [
            pltpu.make_async_copy(
                speeds.at[step, :, pl.ds(lo, hi - lo), :, pl.ds(half * LANES, LANES)],
                speed.at[step, :, pl.ds(lo, hi - lo), half],
                load_sem.at[i, half],
            )
            for half in range(2)
        ]

    own = pltpu.make_async_copy(own_list, own_v, local_sem.at[0])
    own.start()
    blocks = pltpu.make_async_copy(land, mask, local_sem.at[1])
    blocks.start()
    upper = load_x(0, 0, 3) + load_speed(1, 0, 0, 3)
    deep = load_x(2, 3, 8) + load_speed(3, 0, 3, 8)
    late_low = load_speed(4, 1, 0, 2)
    late_high = load_speed(5, 1, 2, 8)
    for c in upper + deep + late_low + late_high:
        c.start()

    blocks.wait()
    for half in range(2):
        for s in range(STRIPS):
            ocean_v[half, 8 * s : 8 * s + 8, :] = jnp.full((8, LANES), mask[half, s].astype(F32))
    own.wait()
    lists[gx] = jnp.full((8, LANES), -1, jnp.int32)
    lists[gx, :, 0:SLOTS] = jnp.broadcast_to(own_v[...], (8, SLOTS))

    def send_edges(e):
        return [
            pltpu.make_async_remote_copy(
                cols.at[e, 0], cols_in.at[e, 0], send_sem.at[e, 0], recv_sem.at[e, 0],
                device_id=(gy, east_at), device_id_type=MESH,
            ),
            pltpu.make_async_remote_copy(
                cols.at[e, 1], cols_in.at[e, 1], send_sem.at[e, 1], recv_sem.at[e, 1],
                device_id=(gy, west_at), device_id_type=MESH,
            ),
            pltpu.make_async_remote_copy(
                rows.at[e, 0], rows_in.at[e, 1 - top], send_sem.at[e, 2], recv_sem.at[e, 3 - top],
                device_id=(north_row, north_col), device_id_type=MESH,
            ),
        ]

    def send_south(e):
        return pltpu.make_async_remote_copy(
            rows.at[e, 1], rows_in.at[e, 0], send_sem.at[e, 3], recv_sem.at[e, 2],
            device_id=(gy - 1, gx), device_id_type=MESH,
        )

    def start_edges(e):
        for c in send_edges(e):
            c.start()

        @pl.when(gy > 0)
        def _():
            send_south(e).start()

    def wait_edges(e):
        for side, peer in ((0, east_at), (1, west_at)):
            pltpu.make_async_remote_copy(
                cols.at[e, side], cols_in.at[e, side], send_sem.at[e, side], recv_sem.at[e, side],
                device_id=(gy, peer), device_id_type=MESH,
            ).wait_recv()
        pltpu.make_async_remote_copy(
            rows.at[e, 0], rows_in.at[e, 0], send_sem.at[e, 2], recv_sem.at[e, 2],
            device_id=(north_row, north_col), device_id_type=MESH,
        ).wait_recv()

        @pl.when(gy > 0)
        def _():
            pltpu.make_async_remote_copy(
                rows.at[e, 0], rows_in.at[e, 1], send_sem.at[e, 2], recv_sem.at[e, 3],
                device_id=(north_row, north_col), device_id_type=MESH,
            ).wait_recv()

    def finish_edges(e):
        for c in send_edges(e):
            c.wait_send()

        @pl.when(gy > 0)
        def _():
            send_south(e).wait_send()

    for c in upper:
        c.wait()
    pack(x, speed.at[0], 0, range(0, 3), cols, rows)
    advance(x, speed.at[0], ocean_v, 0, 3)
    pl.semaphore_wait(barrier, COLUMNS - 1 + (1 - top) + inner)
    start_edges(0)

    def list_copy(peer, slot):
        return pltpu.make_async_remote_copy(
            lists.at[gx], lists.at[slot], list_send.at[peer], list_recv.at[slot],
            device_id=(gy, peer), device_id_type=MESH,
        )

    def send_list(d, _):
        list_copy(lax.rem(gx + 1 + d, COLUMNS), gx).start()
        return 0

    lax.fori_loop(0, COLUMNS - 1, send_list, 0)

    def fill(e, levels):
        wait_edges(e)
        unpack(x, e, levels, cols, rows, cols_in, rows_in, edge, ocean_v, flows, top, gy > 0)

    def settle(e, m, first, last, resumed, dens_ref, surf_ref):
        settle_levels(x, edge.at[e], mix.at[m], ocean_v, first, last, resumed, dens_ref, surf_ref)

    for c in deep:
        c.wait()
    pack(x, speed.at[0], 1, range(3, 8), cols, rows)
    start_edges(1)
    advance(x, speed.at[0], ocean_v, 3, 8)

    fill(0, range(0, 3))
    settle(0, 0, 0, 2, False, None, None)
    for c in late_low:
        c.wait()
    pack(x, speed.at[1], 2, range(0, 2), cols, rows)
    start_edges(2)
    advance(x, speed.at[1], ocean_v, 0, 2)

    fill(1, range(3, 8))
    settle(1, 0, 2, 7, True, None, None)
    for c in late_high:
        c.wait()
    pack(x, speed.at[1], 3, range(2, 8), cols, rows)
    start_edges(3)

    def take_list(d, _):
        peer = lax.rem(gx + 1 + d, COLUMNS)
        list_copy(peer, peer).wait_recv()
        return 0

    lax.fori_loop(0, COLUMNS - 1, take_list, 0)
    send_table(lists, gx, stage, table)
    fetch = pltpu.make_async_copy(table, table_s, local_sem.at[1])
    fetch.start()
    pick_table(lists, gx, picks)

    fill(2, range(0, 2))
    settle(2, 1, 0, 1, False, dens, surf)
    fetch.wait()

    def bucket(peer, target, base):
        tiles = [jnp.clip(table_s[peer, r], 0, SLOTS - 1) for r in range(CAP)]
        blocks = [surf[tile] for tile in tiles]
        for r in range(CAP):
            target[base + r] = blocks[r]

    def relay_copy(peer, slot):
        return pltpu.make_async_remote_copy(
            outgoing.at[pl.ds(peer * CAP, CAP)], incoming.at[pl.ds(slot * CAP, CAP)],
            relay_send.at[peer], relay_recv.at[slot],
            device_id=(gy, peer), device_id_type=MESH,
        )

    def relay_far(d, _):
        peer = (1 - gx // 8) * 8 + lax.rem(gx + d, 8)
        bucket(peer, outgoing, peer * CAP)
        relay_copy(peer, gx).start()
        return 0

    def relay_near(d, _):
        peer = (gx // 8) * 8 + lax.rem(gx + 1 + d, 8)
        bucket(peer, outgoing, peer * CAP)
        relay_copy(peer, gx).start()
        return 0

    lax.fori_loop(0, 8, relay_far, 0)
    lax.fori_loop(0, 7, relay_near, 0)
    bucket(gx, incoming, gx * CAP)

    advance(x, speed.at[1], ocean_v, 2, 8)
    fill(3, range(2, 8))
    settle(3, 1, 1, 7, True, dens, None)

    for e in range(4):
        finish_edges(e)

    def close(d, _):
        peer = lax.rem(gx + 1 + d, COLUMNS)
        list_copy(peer, gx).wait_send()
        relay_copy(peer, gx).wait_send()
        relay_copy(peer, peer).wait_recv()
        return 0

    lax.fori_loop(0, COLUMNS - 1, close, 0)


def output_kernel(x, dens, incoming, picks, tracers_out, dens_out, ice_out, ice, sems):
    copies = []
    for half in range(2):
        lanes = pl.ds(half * LANES, LANES)
        copies.append(
            pltpu.make_async_copy(
                x.at[:, :, half, pl.ds(0, ROWS), :], tracers_out.at[:, :, :, lanes], sems.at[half]
            )
        )
        copies.append(
            pltpu.make_async_copy(
                dens.at[:, half], dens_out.at[:, :, lanes], sems.at[2 + half]
            )
        )
    for c in copies:
        c.start()

    def slot(s, _):
        place = picks[0, s]
        filled = place >= 0
        spot = jnp.clip(place, 0, COLUMNS * CAP - 1)
        heat = jnp.where(filled, incoming[spot, 0], 0.0)
        salt = jnp.where(filled, incoming[spot, 1], 0.0)
        ice[s, 0] = heat
        ice[s, 1] = salt
        ice[s, 2] = density_at(heat, salt, 0)
        return 0

    for part in range(2):
        lax.fori_loop(part * 32, part * 32 + 32, slot, 0, unroll=8)
        c = pltpu.make_async_copy(
            ice.at[pl.ds(part * 32, 32)], ice_out.at[pl.ds(part * 32, 32)], sems.at[4 + part]
        )
        c.start()
        copies.append(c)
    for c in copies:
        c.wait()


def on_device(tracers, face_speeds, ocean_block, ice_blocks):
    anywhere = pl.BlockSpec(memory_space=pl.ANY)
    vmem = pl.BlockSpec(memory_space=pltpu.VMEM)
    smem = pl.BlockSpec(memory_space=pltpu.SMEM)
    hbm = pl.BlockSpec(memory_space=pltpu.HBM)
    dma = pltpu.SemaphoreType.DMA
    x, dens, incoming, picks = pl.pallas_call(
        ocean_kernel,
        out_shape=(
            jax.ShapeDtypeStruct((2, LEVELS, 2, ROWS + 8, LANES), F32),
            jax.ShapeDtypeStruct((LEVELS, 2, ROWS, LANES), F32),
            jax.ShapeDtypeStruct((COLUMNS * CAP, 2, 8, LANES), F32),
            jax.ShapeDtypeStruct((8, LANES), jnp.int32),
        ),
        in_specs=[hbm, hbm, hbm, hbm],
        out_specs=(vmem, vmem, vmem, vmem),
        scratch_shapes=[
            pltpu.VMEM((2, 2, LEVELS, 2, ROWS, LANES), F32),
            pltpu.VMEM((4, 2, 64, LANES), F32),
            pltpu.VMEM((4, 2, 48, LANES), F32),
            pltpu.VMEM((4, 2, 64, LANES), F32),
            pltpu.VMEM((4, 2, 48, LANES), F32),
            pltpu.VMEM((4, ROWS, LANES), F32),
            pltpu.VMEM((2, 2, 2, ROWS, LANES), F32),
            pltpu.VMEM((2, ROWS, LANES), F32),
            pltpu.VMEM((2, 32, LANES), F32),
            pltpu.VMEM((1, SLOTS), jnp.int32),
            pltpu.SMEM((2, STRIPS), jnp.int32),
            pltpu.VMEM((COLUMNS, 8, LANES), jnp.int32),
            pltpu.VMEM((COLUMNS, LANES), jnp.int32),
            pltpu.VMEM((COLUMNS, LANES), jnp.int32),
            pltpu.SMEM((COLUMNS, LANES), jnp.int32),
            pltpu.VMEM((SLOTS, 2, 8, LANES), F32),
            pltpu.VMEM((COLUMNS * CAP, 2, 8, LANES), F32),
            dma((6, 2)),
            dma((4, 4)),
            dma((4, 4)),
            dma((COLUMNS,)),
            dma((COLUMNS,)),
            dma((COLUMNS,)),
            dma((COLUMNS,)),
            dma((2,)),
        ],
        compiler_params=pltpu.CompilerParams(
            collective_id=0, has_side_effects=True, vmem_limit_bytes=20 << 20
        ),
        name="ocean",
    )(*[
        pltpu.with_memory_space_constraint(v, pltpu.HBM)
        for v in (tracers, face_speeds, ocean_block.T, ice_blocks.reshape(1, SLOTS))
    ])
    return pl.pallas_call(
        output_kernel,
        out_shape=(
            jax.ShapeDtypeStruct(tracers.shape, F32),
            jax.ShapeDtypeStruct(tracers.shape[1:], F32),
            jax.ShapeDtypeStruct((SLOTS, 3, 8, LANES), F32),
        ),
        in_specs=[anywhere, anywhere, vmem, smem],
        out_specs=(anywhere, anywhere, anywhere),
        scratch_shapes=[pltpu.VMEM((SLOTS, 3, 8, LANES), F32), dma((6,))],
        compiler_params=pltpu.CompilerParams(vmem_limit_bytes=16 << 20),
        name="outputs",
    )(x, dens, incoming, picks)


def solution(mesh):
    return jax.shard_map(
        on_device,
        mesh=mesh,
        in_specs=(
            P(None, None, "gy", "gx"),
            P(None, None, None, "gy", "gx"),
            P("gy", "gx"),
            P(("gy", "gx")),
        ),
        out_specs=(
            P(None, None, "gy", "gx"),
            P(None, "gy", "gx"),
            P(("gy", "gx"), None, None, None),
        ),
        check_vma=False,
    )
```

```python
import functools

import jax
import jax.numpy as jnp
from jax import lax
from jax.experimental import pallas as pl
from jax.experimental.pallas import tpu as pltpu
from jax.sharding import PartitionSpec as P

MESH = pl.DeviceIdType.MESH
LEVELS = 8
ROWS = 256
LANES = 128
STRIPS = 32
CHUNK = 64
COLUMNS = 16
TOP = 7
CAP = 8
SLOTS = 64
FACES = 24
F32 = jnp.float32

warming_swell_coefficient = 0.1655
haline_base = 0.7655
warming_swell_quadratic = 0.05952
haline_curve = 0.00054914
warming_compression_coupling = 0.0001497
haline_press = 1.109e-05
mixing_contraction_coefficient = 0.0024341
lateral_mix = 0.08
mixing_base = 0.05
mixing_boost = 0.2


def density_at(heat, salt, level):
    depth = 10.0 * level + 5.0
    heat_one = -warming_swell_coefficient * (1.0 + warming_compression_coupling * depth)
    heat_two = -warming_swell_coefficient * 0.5 * warming_swell_quadratic
    salt_one = haline_base * (1.0 - haline_press * depth)
    salt_two = -haline_base * 0.5 * haline_curve
    return heat * (
        heat_one + heat_two * heat - mixing_contraction_coefficient * salt
    ) + salt * (salt_one + salt_two * salt)


def face_weights(speed):
    lower = jnp.maximum(speed, 0.0) + lateral_mix
    return lower, speed - lower


def face_flux(speed, lower_cells, upper_cells):
    lower, upper = face_weights(speed)
    return lower * lower_cells + upper * upper_cells


def advance(x, speed, ocean_v, low, high):
    lane = lax.broadcasted_iota(jnp.int32, (ROWS, LANES), 1)
    first_lane, last_lane = lane == 0, lane == LANES - 1
    last_row = lax.broadcasted_iota(jnp.int32, (8, LANES), 0) == 7
    here, above = pl.ds(0, ROWS), pl.ds(1, ROWS)

    def level(k, _):
        east = [face_weights(speed[0, k, half]) for half in range(2)]
        north = [face_weights(speed[1, k, half]) for half in range(2)]
        for t in range(2):
            cells = [x[t, k, half, here, :] for half in range(2)]
            turned = [pltpu.roll(c, LANES - 1, 1) for c in cells]
            eastern = [jnp.where(last_lane, turned[1], turned[0]), turned[1]]
            ef = [east[half][0] * cells[half] + east[half][1] * eastern[half] for half in range(2)]
            ef[1] = jnp.where(last_lane, 0.0, ef[1])
            back = [pltpu.roll(f, 1, 1) for f in ef]
            wf = [jnp.where(first_lane, 0.0, back[0]), jnp.where(first_lane, back[0], back[1])]
            for half in range(2):
                nf = north[half][0] * cells[half] + north[half][1] * x[t, k, half, above, :]
                nf = jnp.concatenate(
                    [nf[: ROWS - 8], jnp.where(last_row, 0.0, nf[ROWS - 8 :])], axis=0
                )
                change = (ef[half] - wf[half]) + (nf - pltpu.roll(nf, 1, 0))
                x[t, k, half, here, :] = cells[half] - ocean_v[half] * change
        return 0

    lax.fori_loop(low, high, level, 0)


def settle_levels(x, edge, mix, ocean_v, first, last, resumed, dens, surf):
    lane = lax.broadcasted_iota(jnp.int32, (CHUNK, LANES), 1)
    first_lane, last_lane = lane == 0, lane == LANES - 1

    def chunk(c, _):
        here = pl.ds(pl.multiple_of(c * CHUNK, CHUNK), CHUNK)
        rim = edge[here, :]
        ocean = [ocean_v[half, here, :] for half in range(2)]

        def advected(k):
            out = []
            for t in range(2):
                ends = pltpu.roll(rim, LANES - 1 - 2 * (t * LEVELS + k), 1)
                out.append(
                    [
                        x[t, k, 0, here, :] + jnp.where(first_lane, ends, 0.0),
                        x[t, k, 1, here, :] + jnp.where(last_lane, ends, 0.0),
                    ]
                )
            return out

        def settle(k, adv, flux, over):
            for half in range(2):
                done = []
                for t in range(2):
                    if flux is None:
                        gain = -over[t][half]
                    elif over is None:
                        gain = flux[t][half]
                    else:
                        gain = flux[t][half] - over[t][half]
                    value = adv[t][half] + ocean[half] * gain
                    x[t, k, half, here, :] = value
                    done.append(value)
                    if surf is not None and k == 0:
                        for i in range(CHUNK // 8):
                            tile = 2 * (c * (CHUNK // 8) + i) + half
                            surf[tile, t] = value[8 * i : 8 * i + 8]
                if dens is not None:
                    dens[k, half, here, :] = density_at(done[0], done[1], k)

        over = None
        if resumed:
            adv = [[x[t, first, half, here, :] for half in range(2)] for t in range(2)]
            over = [[mix[t, half, here, :] for half in range(2)] for t in range(2)]
        else:
            adv = advected(first)
        rho = [density_at(adv[0][half], adv[1][half], first) for half in range(2)]
        for k in range(first + 1, last + 1):
            lower = advected(k)
            rho_lower = [density_at(lower[0][half], lower[1][half], k) for half in range(2)]
            flux = [[None, None], [None, None]]
            for half in range(2):
                kappa = (mixing_base + 0.5 * mixing_boost) - 0.5 * mixing_boost * jnp.tanh(
                    rho_lower[half] - rho[half]
                )
                for t in range(2):
                    flux[t][half] = kappa * (lower[t][half] - adv[t][half])
            settle(k - 1, adv, flux, over)
            adv, rho, over = lower, rho_lower, flux
        if last == LEVELS - 1:
            settle(last, adv, None, over)
        else:
            for t in range(2):
                for half in range(2):
                    x[t, last, half, here, :] = adv[t][half]
                    mix[t, half, here, :] = over[t][half]
        return 0

    lax.fori_loop(0, ROWS // CHUNK, chunk, 0)


def aligned(index):
    return index if isinstance(index, int) else pl.multiple_of(index, 8)


def groups(body, count):
    if count <= 3:
        for g in range(8):
            body(g, 0)
    else:
        lax.fori_loop(0, 8, body, 0, unroll=4)


def pack_faces(speed, faces, levels, rows_list):
    lane = lax.broadcasted_iota(jnp.int32, (8, LANES), 1)

    def group(g, _):
        parts = []
        for q in range(4):
            here = pl.ds(aligned(g * 32 + q * 8), 8)
            face = jnp.zeros((8, LANES), F32)
            for k in levels:
                spot = 32 * q + 2 * k + 1
                value = pltpu.roll(speed[0, k, 1, here, :], spot + 1, 1)
                face = jnp.where(lane == spot, value, face)
            parts.append(face)
        face = (parts[0] + parts[1]) + (parts[2] + parts[3])
        faces[pl.ds(aligned(g * 8), 8), :] = face + pltpu.roll(face, 2 * LEVELS, 1)
        return 0

    groups(group, len(levels))
    for k in levels:
        for half in range(2):
            spot = 32 + k * 2 + half
            for rows in rows_list:
                rows[spot : spot + 1, :] = speed[1, k, half, ROWS - 1 : ROWS, :]


def pack(x, faces, e, levels, cols, rows):
    lane = lax.broadcasted_iota(jnp.int32, (8, LANES), 1)
    pair = lane >> 1
    odd = (lane & 1) != 0

    def group(g, _):
        parts = []
        for q in range(4):
            here = pl.ds(aligned(g * 32 + q * 8), 8)
            both = jnp.zeros((8, LANES), F32)
            for k in levels:
                for t in range(2):
                    spot = 16 * q + t * LEVELS + k
                    ends = jnp.where(lane == 0, x[t, k, 0, here, :], x[t, k, 1, here, :])
                    both = jnp.where(pair == spot, pltpu.roll(ends, 2 * spot + 1, 1), both)
            parts.append(both)
        both = (parts[0] + parts[1]) + (parts[2] + parts[3])
        here = pl.ds(aligned(g * 8), 8)
        cols[e, 0, here, :] = jnp.where(odd, faces[here, :], both)
        cols[e, 1, here, :] = both
        return 0

    groups(group, len(levels))
    for k in levels:
        for half in range(2):
            for t in range(2):
                spot = t * 16 + k * 2 + half
                rows[e, 0, spot : spot + 1, :] = x[t, k, half, ROWS - 1 : ROWS, :]
                rows[e, 1, spot : spot + 1, :] = x[t, k, half, 0:1, :]


def reversed_lanes(value):
    lane = lax.broadcasted_iota(jnp.int32, value.shape, 1)
    for bit in (1, 2, 4, 8, 16, 32, 64):
        upper = (lane & bit) != 0
        value = jnp.where(
            upper, pltpu.roll(value, bit, 1), pltpu.roll(value, LANES - bit, 1)
        )
    return value


def unpack(x, e, levels, cols, rows, cols_in, rows_in, edge, ocean_v, flows, top, open_south):
    odd = (lax.broadcasted_iota(jnp.int32, (8, LANES), 1) & 1) != 0
    for g in range(8):
        here = pl.ds(g * 8, 8)
        arrived = cols_in[e, 0, here, :]
        fw = face_flux(arrived, pltpu.roll(arrived, 1, 1), cols[e, 1, here, :])
        own, arrived = cols[e, 0, here, :], cols_in[e, 1, here, :]
        fe = face_flux(pltpu.roll(own, LANES - 1, 1), own, pltpu.roll(arrived, LANES - 1, 1))
        both = jnp.where(odd, fw, -fe)
        for q in range(4):
            here = pl.ds(g * 32 + q * 8, 8)
            ocean = jnp.where(odd, ocean_v[0, here, :], ocean_v[1, here, :])
            edge[e, here, :] = (pltpu.roll(both, LANES - 32 * q, 1) if q else both) * ocean

    right = (lax.broadcasted_iota(jnp.int32, (16, LANES), 0) & 1) != 0
    low = jnp.where(right, ocean_v[1, 0:1, :], ocean_v[0, 0:1, :])
    high = jnp.where(right, ocean_v[1, ROWS - 1 : ROWS, :], ocean_v[0, ROWS - 1 : ROWS, :])
    speed = rows_in[e, 1, 32:48, :]
    for t in range(2):
        part = pl.ds(16 * t, 16)
        flux = face_flux(speed, rows_in[e, 1, part, :], rows[e, 1, part, :])
        flows[0, part, :] = jnp.where(open_south, low * flux, 0.0)

    def north(arrived):
        for t in range(2):
            part = pl.ds(16 * t, 16)
            flux = face_flux(rows[e, 0, 32:48, :], rows[e, 0, part, :], arrived[16 * t : 16 * t + 16])
            flows[1, part, :] = -high * flux

    @pl.when(top == 0)
    def _():
        north(rows_in[e, 0, 0:32, :])

    @pl.when(top == 1)
    def _():
        value = reversed_lanes(rows_in[e, 0, 0:32, :])
        odd_row = (lax.broadcasted_iota(jnp.int32, (32, LANES), 0) & 1) != 0
        north(jnp.where(odd_row, pltpu.roll(value, 1, 0), pltpu.roll(value, 31, 0)))

    for k in levels:
        for half in range(2):
            for t in range(2):
                spot = t * 16 + k * 2 + half
                x[t, k, half, 0:1, :] += flows[0, spot : spot + 1, :]
                x[t, k, half, ROWS - 1 : ROWS, :] += flows[1, spot : spot + 1, :]


def running_count(flags):
    lane = lax.broadcasted_iota(jnp.int32, flags.shape, 1)
    total = flags
    for shift in (1, 2, 4, 8, 16, 32):
        total = total + jnp.where(lane >= shift, pltpu.roll(total, shift, 1), 0)
    return total - flags


def lane_total(value):
    for shift in (1, 2, 4, 8, 16, 32, 64):
        value = value + pltpu.roll(value, shift, 1)
    return value


def send_table(lists, gx, stage, table):
    for p in range(COLUMNS):
        stage[p : p + 1, :] = lists[p, 0:1, :]
    ids = stage[...]
    lane = lax.broadcasted_iota(jnp.int32, ids.shape, 1)
    mine = ((ids & 31) >> 1 == gx) & (ids >= 0)
    rank = running_count(jnp.where(mine, 1, 0))
    tile = ((ids >> 5) & (STRIPS - 1)) * 2 + (ids & 1)
    out = jnp.zeros_like(ids)
    for r in range(CAP):
        found = lane_total(jnp.where(mine & (rank == r), tile, 0))
        out = jnp.where(lane == r, found, out)
    table[...] = out


def pick_table(lists, gx, out):
    ids = jnp.broadcast_to(lists[gx, 0:1, :], (COLUMNS, LANES))
    row = lax.broadcasted_iota(jnp.int32, ids.shape, 0)
    mine = ((ids & 31) >> 1 == row) & (ids >= 0)
    flags = jnp.where(mine, 1, 0)
    place = jnp.where(mine, running_count(flags) + row * CAP + 1, 0)
    both = place[0:8] + place[8:16]
    for shift in (4, 2, 1):
        both = both + pltpu.roll(both, shift, 0)
    out[...] = both - 1


def ocean_kernel(
    tracers, speeds, land, own_list, x, dens, incoming, picks,
    speed, cols, rows, cols_in, rows_in, edge, mix, ocean_v, flows, faces, own_v, mask,
    lists, stage, table, table_s, surf, outgoing,
    load_sem, send_sem, recv_sem, list_send, list_recv, relay_send, relay_recv, local_sem,
):
    gy, gx = lax.axis_index("gy"), lax.axis_index("gx")
    top = gy // TOP
    inner = (gy + TOP - 1) // TOP
    east_at = lax.rem(gx + 1, COLUMNS)
    west_at = lax.rem(gx + COLUMNS - 1, COLUMNS)
    north_row = gy + 1 - top
    north_col = gx + top * (COLUMNS - 1 - 2 * gx)

    barrier = pltpu.get_barrier_semaphore()

    def greet(d, _):
        peer = lax.rem(gx + 1 + d, COLUMNS)
        pl.semaphore_signal(barrier, inc=1, device_id=(gy, peer), device_id_type=MESH)
        return 0

    lax.fori_loop(0, COLUMNS - 1, greet, 0)

    @pl.when(gy < TOP)
    def _():
        pl.semaphore_signal(barrier, inc=1, device_id=(gy + 1, gx), device_id_type=MESH)

    @pl.when(gy > 0)
    def _():
        pl.semaphore_signal(barrier, inc=1, device_id=(gy - 1, gx), device_id_type=MESH)

    def load_x(i, lo, hi):
        return [
            pltpu.make_async_copy(
                tracers.at[:, pl.ds(lo, hi - lo), :, pl.ds(half * LANES, LANES)],
                x.at[:, pl.ds(lo, hi - lo), half, pl.ds(0, ROWS), :],
                load_sem.at[i, half],
            )
            for half in range(2)
        ]

    def load_speed(i, step, lo, hi):
        return [
            pltpu.make_async_copy(
                speeds.at[step, :, pl.ds(lo, hi - lo), :, pl.ds(half * LANES, LANES)],
                speed.at[step, :, pl.ds(lo, hi - lo), half],
                load_sem.at[i, half],
            )
            for half in range(2)
        ]

    own = pltpu.make_async_copy(own_list, own_v, local_sem.at[0])
    own.start()
    blocks = pltpu.make_async_copy(land, mask, local_sem.at[1])
    blocks.start()
    upper = load_x(0, 0, 3) + load_speed(1, 0, 0, 3)
    deep = load_x(2, 3, 8) + load_speed(3, 0, 3, 8)
    late_low = load_speed(4, 1, 0, 2)
    late_high = load_speed(5, 1, 2, 8)
    for c in upper + deep + late_low + late_high:
        c.start()

    blocks.wait()
    for half in range(2):
        for s in range(STRIPS):
            ocean_v[half, 8 * s : 8 * s + 8, :] = jnp.full((8, LANES), mask[half, s].astype(F32))
    own.wait()
    lists[gx] = jnp.full((8, LANES), -1, jnp.int32)
    lists[gx, :, 0:SLOTS] = jnp.broadcast_to(own_v[...], (8, SLOTS))

    def send_edges(e):
        return [
            pltpu.make_async_remote_copy(
                cols.at[e, 0], cols_in.at[e, 0], send_sem.at[e, 0], recv_sem.at[e, 0],
                device_id=(gy, east_at), device_id_type=MESH,
            ),
            pltpu.make_async_remote_copy(
                cols.at[e, 1], cols_in.at[e, 1], send_sem.at[e, 1], recv_sem.at[e, 1],
                device_id=(gy, west_at), device_id_type=MESH,
            ),
            pltpu.make_async_remote_copy(
                rows.at[e, 0], rows_in.at[e, 1 - top], send_sem.at[e, 2], recv_sem.at[e, 3 - top],
                device_id=(north_row, north_col), device_id_type=MESH,
            ),
        ]

    def send_south(e):
        return pltpu.make_async_remote_copy(
            rows.at[e, 1], rows_in.at[e, 0], send_sem.at[e, 3], recv_sem.at[e, 2],
            device_id=(gy - 1, gx), device_id_type=MESH,
        )

    def start_edges(e):
        for c in send_edges(e):
            c.start()

        @pl.when(gy > 0)
        def _():
            send_south(e).start()

    def wait_edges(e):
        for side, peer in ((0, east_at), (1, west_at)):
            pltpu.make_async_remote_copy(
                cols.at[e, side], cols_in.at[e, side], send_sem.at[e, side], recv_sem.at[e, side],
                device_id=(gy, peer), device_id_type=MESH,
            ).wait_recv()
        pltpu.make_async_remote_copy(
            rows.at[e, 0], rows_in.at[e, 0], send_sem.at[e, 2], recv_sem.at[e, 2],
            device_id=(north_row, north_col), device_id_type=MESH,
        ).wait_recv()

        @pl.when(gy > 0)
        def _():
            pltpu.make_async_remote_copy(
                rows.at[e, 0], rows_in.at[e, 1], send_sem.at[e, 2], recv_sem.at[e, 3],
                device_id=(north_row, north_col), device_id_type=MESH,
            ).wait_recv()

    def finish_edges(e):
        for c in send_edges(e):
            c.wait_send()

        @pl.when(gy > 0)
        def _():
            send_south(e).wait_send()

    for c in upper:
        c.wait()
    pack_faces(speed.at[0], faces.at[0], range(0, 3), [rows.at[0, 0]])
    pack(x, faces.at[0], 0, range(0, 3), cols, rows)
    advance(x, speed.at[0], ocean_v, 0, 3)
    pl.semaphore_wait(barrier, COLUMNS - 1 + (1 - top) + inner)
    start_edges(0)

    def list_copy(peer, slot):
        return pltpu.make_async_remote_copy(
            lists.at[gx], lists.at[slot], list_send.at[peer], list_recv.at[slot],
            device_id=(gy, peer), device_id_type=MESH,
        )

    def send_list(d, _):
        list_copy(lax.rem(gx + 1 + d, COLUMNS), gx).start()
        return 0

    lax.fori_loop(0, COLUMNS - 1, send_list, 0)

    def fill(e, levels):
        wait_edges(e)
        unpack(x, e, levels, cols, rows, cols_in, rows_in, edge, ocean_v, flows, top, gy > 0)

    def settle(e, m, first, last, resumed, dens_ref, surf_ref):
        settle_levels(x, edge.at[e], mix.at[m], ocean_v, first, last, resumed, dens_ref, surf_ref)

    for c in deep:
        c.wait()
    pack_faces(speed.at[0], faces.at[1], range(3, 8), [rows.at[1, 0]])
    pack(x, faces.at[1], 1, range(3, 8), cols, rows)
    start_edges(1)
    advance(x, speed.at[0], ocean_v, 3, 8)
    for c in late_low + late_high:
        c.wait()
    pack_faces(speed.at[1], faces.at[2], range(0, 8), [rows.at[2, 0], rows.at[3, 0]])

    fill(0, range(0, 3))
    settle(0, 0, 0, 2, False, None, None)
    pack(x, faces.at[2], 2, range(0, 2), cols, rows)
    start_edges(2)
    advance(x, speed.at[1], ocean_v, 0, 2)

    fill(1, range(3, 8))
    settle(1, 0, 2, 7, True, None, None)
    pack(x, faces.at[2], 3, range(2, 8), cols, rows)
    start_edges(3)

    def take_list(d, _):
        peer = lax.rem(gx + 1 + d, COLUMNS)
        list_copy(peer, peer).wait_recv()
        return 0

    lax.fori_loop(0, COLUMNS - 1, take_list, 0)
    send_table(lists, gx, stage, table)
    fetch = pltpu.make_async_copy(table, table_s, local_sem.at[1])
    fetch.start()

    fill(2, range(0, 2))
    settle(2, 1, 0, 1, False, dens, surf)
    fetch.wait()

    def bucket(peer, target, base):
        tiles = [jnp.clip(table_s[peer, r], 0, SLOTS - 1) for r in range(CAP)]
        blocks = [surf[tile] for tile in tiles]
        for r in range(CAP):
            target[base + r] = blocks[r]

    def relay_copy(peer, slot):
        return pltpu.make_async_remote_copy(
            outgoing.at[pl.ds(peer * CAP, CAP)], incoming.at[pl.ds(slot * CAP, CAP)],
            relay_send.at[peer], relay_recv.at[slot],
            device_id=(gy, peer), device_id_type=MESH,
        )

    def relay_far(d, _):
        peer = (1 - gx // 8) * 8 + lax.rem(gx + d + 4, 8)
        bucket(peer, outgoing, peer * CAP)
        relay_copy(peer, gx).start()
        return 0

    def relay_near(d, _):
        peer = (gx // 8) * 8 + lax.rem(gx + 1 + d, 8)
        bucket(peer, outgoing, peer * CAP)
        relay_copy(peer, gx).start()
        return 0

    lax.fori_loop(0, 8, relay_far, 0)
    lax.fori_loop(0, 7, relay_near, 0)
    bucket(gx, incoming, gx * CAP)
    pick_table(lists, gx, picks)

    advance(x, speed.at[1], ocean_v, 2, 8)
    fill(3, range(2, 8))
    settle(3, 1, 1, 7, True, dens, None)

    for e in range(4):
        finish_edges(e)

    def close(d, _):
        peer = lax.rem(gx + 1 + d, COLUMNS)
        list_copy(peer, gx).wait_send()
        relay_copy(peer, gx).wait_send()
        relay_copy(peer, peer).wait_recv()
        return 0

    lax.fori_loop(0, COLUMNS - 1, close, 0)


def output_kernel(x, dens, incoming, picks, tracers_out, dens_out, ice_out, ice, sems):
    copies = []
    for half in range(2):
        lanes = pl.ds(half * LANES, LANES)
        copies.append(
            pltpu.make_async_copy(
                x.at[:, :, half, pl.ds(0, ROWS), :], tracers_out.at[:, :, :, lanes], sems.at[half]
            )
        )
        copies.append(
            pltpu.make_async_copy(
                dens.at[:, half], dens_out.at[:, :, lanes], sems.at[2 + half]
            )
        )
    for c in copies:
        c.start()

    def slot(s, _):
        place = picks[0, s]
        filled = place >= 0
        spot = jnp.clip(place, 0, COLUMNS * CAP - 1)
        heat = jnp.where(filled, incoming[spot, 0], 0.0)
        salt = jnp.where(filled, incoming[spot, 1], 0.0)
        ice[s, 0] = heat
        ice[s, 1] = salt
        ice[s, 2] = density_at(heat, salt, 0)
        return 0

    for part in range(2):
        lax.fori_loop(part * 32, part * 32 + 32, slot, 0, unroll=8)
        c = pltpu.make_async_copy(
            ice.at[pl.ds(part * 32, 32)], ice_out.at[pl.ds(part * 32, 32)], sems.at[4 + part]
        )
        c.start()
        copies.append(c)
    for c in copies:
        c.wait()


def on_device(tracers, face_speeds, ocean_block, ice_blocks):
    anywhere = pl.BlockSpec(memory_space=pl.ANY)
    vmem = pl.BlockSpec(memory_space=pltpu.VMEM)
    smem = pl.BlockSpec(memory_space=pltpu.SMEM)
    hbm = pl.BlockSpec(memory_space=pltpu.HBM)
    dma = pltpu.SemaphoreType.DMA
    x, dens, incoming, picks = pl.pallas_call(
        ocean_kernel,
        out_shape=(
            jax.ShapeDtypeStruct((2, LEVELS, 2, ROWS + 8, LANES), F32),
            jax.ShapeDtypeStruct((LEVELS, 2, ROWS, LANES), F32),
            jax.ShapeDtypeStruct((COLUMNS * CAP, 2, 8, LANES), F32),
            jax.ShapeDtypeStruct((8, LANES), jnp.int32),
        ),
        in_specs=[hbm, hbm, hbm, hbm],
        out_specs=(vmem, vmem, vmem, vmem),
        scratch_shapes=[
            pltpu.VMEM((2, 2, LEVELS, 2, ROWS, LANES), F32),
            pltpu.VMEM((4, 2, 64, LANES), F32),
            pltpu.VMEM((4, 2, 48, LANES), F32),
            pltpu.VMEM((4, 2, 64, LANES), F32),
            pltpu.VMEM((4, 2, 48, LANES), F32),
            pltpu.VMEM((4, ROWS, LANES), F32),
            pltpu.VMEM((2, 2, 2, ROWS, LANES), F32),
            pltpu.VMEM((2, ROWS, LANES), F32),
            pltpu.VMEM((2, 32, LANES), F32),
            pltpu.VMEM((3, 64, LANES), F32),
            pltpu.VMEM((1, SLOTS), jnp.int32),
            pltpu.SMEM((2, STRIPS), jnp.int32),
            pltpu.VMEM((COLUMNS, 8, LANES), jnp.int32),
            pltpu.VMEM((COLUMNS, LANES), jnp.int32),
            pltpu.VMEM((COLUMNS, LANES), jnp.int32),
            pltpu.SMEM((COLUMNS, LANES), jnp.int32),
            pltpu.VMEM((SLOTS, 2, 8, LANES), F32),
            pltpu.VMEM((COLUMNS * CAP, 2, 8, LANES), F32),
            dma((6, 2)),
            dma((4, 4)),
            dma((4, 4)),
            dma((COLUMNS,)),
            dma((COLUMNS,)),
            dma((COLUMNS,)),
            dma((COLUMNS,)),
            dma((2,)),
        ],
        compiler_params=pltpu.CompilerParams(
            collective_id=0, has_side_effects=True, vmem_limit_bytes=20 << 20
        ),
        name="ocean",
    )(*[
        pltpu.with_memory_space_constraint(v, pltpu.HBM)
        for v in (tracers, face_speeds, ocean_block.T, ice_blocks.reshape(1, SLOTS))
    ])
    return pl.pallas_call(
        output_kernel,
        out_shape=(
            jax.ShapeDtypeStruct(tracers.shape, F32),
            jax.ShapeDtypeStruct(tracers.shape[1:], F32),
            jax.ShapeDtypeStruct((SLOTS, 3, 8, LANES), F32),
        ),
        in_specs=[anywhere, anywhere, vmem, smem],
        out_specs=(anywhere, anywhere, anywhere),
        scratch_shapes=[pltpu.VMEM((SLOTS, 3, 8, LANES), F32), dma((6,))],
        compiler_params=pltpu.CompilerParams(vmem_limit_bytes=16 << 20),
        name="outputs",
    )(x, dens, incoming, picks)


def solution(mesh):
    return jax.shard_map(
        on_device,
        mesh=mesh,
        in_specs=(
            P(None, None, "gy", "gx"),
            P(None, None, None, "gy", "gx"),
            P("gy", "gx"),
            P(("gy", "gx")),
        ),
        out_specs=(
            P(None, None, "gy", "gx"),
            P(None, "gy", "gx"),
            P(("gy", "gx"), None, None, None),
        ),
        check_vma=False,
    )
```

```python
import functools

import jax
import jax.numpy as jnp
from jax import lax
from jax.experimental import pallas as pl
from jax.experimental.pallas import tpu as pltpu
from jax.sharding import PartitionSpec as P

MESH = pl.DeviceIdType.MESH
LEVELS = 8
ROWS = 256
LANES = 128
STRIPS = 32
RELAY = ((1, 4), (1, 5), (0, 4), (1, 6), (1, 7), (0, 5), (1, 0), (1, 1), (0, 3), (1, 2), (1, 3), (0, 6), (0, 2), (0, 7), (0, 1))
COLUMNS = 16
TOP = 7
CAP = 8
SLOTS = 64
FACES = 24
F32 = jnp.float32

warming_swell_coefficient = 0.1655
haline_base = 0.7655
warming_swell_quadratic = 0.05952
haline_curve = 0.00054914
warming_compression_coupling = 0.0001497
haline_press = 1.109e-05
mixing_contraction_coefficient = 0.0024341
lateral_mix = 0.08
mixing_base = 0.05
mixing_boost = 0.2


def density_at(heat, salt, level):
    depth = 10.0 * level + 5.0
    heat_one = -warming_swell_coefficient * (1.0 + warming_compression_coupling * depth)
    heat_two = -warming_swell_coefficient * 0.5 * warming_swell_quadratic
    salt_one = haline_base * (1.0 - haline_press * depth)
    salt_two = -haline_base * 0.5 * haline_curve
    return heat * (
        heat_one + heat_two * heat - mixing_contraction_coefficient * salt
    ) + salt * (salt_one + salt_two * salt)


def face_weights(speed):
    lower = jnp.maximum(speed, 0.0) + lateral_mix
    return lower, speed - lower


def face_flux(speed, lower_cells, upper_cells):
    lower, upper = face_weights(speed)
    return lower * lower_cells + upper * upper_cells


def advance(x, speed, ocean_v, low, high):
    lane = lax.broadcasted_iota(jnp.int32, (ROWS, LANES), 1)
    first_lane, last_lane = lane == 0, lane == LANES - 1
    last_row = lax.broadcasted_iota(jnp.int32, (8, LANES), 0) == 7
    here, above = pl.ds(0, ROWS), pl.ds(1, ROWS)

    def level(k, _):
        east = [face_weights(speed[0, k, half]) for half in range(2)]
        north = [face_weights(speed[1, k, half]) for half in range(2)]
        for t in range(2):
            cells = [x[t, k, half, here, :] for half in range(2)]
            turned = [pltpu.roll(c, LANES - 1, 1) for c in cells]
            eastern = [jnp.where(last_lane, turned[1], turned[0]), turned[1]]
            ef = [east[half][0] * cells[half] + east[half][1] * eastern[half] for half in range(2)]
            ef[1] = jnp.where(last_lane, 0.0, ef[1])
            back = [pltpu.roll(f, 1, 1) for f in ef]
            wf = [jnp.where(first_lane, 0.0, back[0]), jnp.where(first_lane, back[0], back[1])]
            for half in range(2):
                nf = north[half][0] * cells[half] + north[half][1] * x[t, k, half, above, :]
                nf = jnp.concatenate(
                    [nf[: ROWS - 8], jnp.where(last_row, 0.0, nf[ROWS - 8 :])], axis=0
                )
                change = (ef[half] - wf[half]) + (nf - pltpu.roll(nf, 1, 0))
                x[t, k, half, here, :] = cells[half] - ocean_v[half] * change
        return 0

    lax.fori_loop(low, high, level, 0)


def settle_levels(x, edge, mix, ocean_v, first, last, resumed, dens, surf, size):
    lane = lax.broadcasted_iota(jnp.int32, (size, LANES), 1)
    first_lane, last_lane = lane == 0, lane == LANES - 1

    def chunk(c, _):
        here = pl.ds(aligned(c * size), size)
        rim = edge[here, :]
        ocean = [ocean_v[half, here, :] for half in range(2)]

        def advected(k):
            out = []
            for t in range(2):
                ends = pltpu.roll(rim, LANES - 1 - 2 * (t * LEVELS + k), 1)
                out.append(
                    [
                        x[t, k, 0, here, :] + jnp.where(first_lane, ends, 0.0),
                        x[t, k, 1, here, :] + jnp.where(last_lane, ends, 0.0),
                    ]
                )
            return out

        def settle(k, adv, flux, over):
            for half in range(2):
                done = []
                for t in range(2):
                    if flux is None:
                        gain = -over[t][half]
                    elif over is None:
                        gain = flux[t][half]
                    else:
                        gain = flux[t][half] - over[t][half]
                    value = adv[t][half] + ocean[half] * gain
                    x[t, k, half, here, :] = value
                    done.append(value)
                    if surf is not None and k == 0:
                        for i in range(size // 8):
                            tile = 2 * (c * (size // 8) + i) + half
                            surf[tile, t] = value[8 * i : 8 * i + 8]
                if dens is not None:
                    dens[k, half, here, :] = density_at(done[0], done[1], k)

        over = None
        if resumed:
            adv = [[x[t, first, half, here, :] for half in range(2)] for t in range(2)]
            over = [[mix[t, half, here, :] for half in range(2)] for t in range(2)]
        else:
            adv = advected(first)
        rho = [density_at(adv[0][half], adv[1][half], first) for half in range(2)]
        for k in range(first + 1, last + 1):
            lower = advected(k)
            rho_lower = [density_at(lower[0][half], lower[1][half], k) for half in range(2)]
            flux = [[None, None], [None, None]]
            for half in range(2):
                kappa = (mixing_base + 0.5 * mixing_boost) - 0.5 * mixing_boost * jnp.tanh(
                    rho_lower[half] - rho[half]
                )
                for t in range(2):
                    flux[t][half] = kappa * (lower[t][half] - adv[t][half])
            settle(k - 1, adv, flux, over)
            adv, rho, over = lower, rho_lower, flux
        if last == LEVELS - 1:
            settle(last, adv, None, over)
        else:
            for t in range(2):
                for half in range(2):
                    x[t, last, half, here, :] = adv[t][half]
                    mix[t, half, here, :] = over[t][half]
        return 0

    if size == ROWS:
        chunk(0, 0)
    else:
        lax.fori_loop(0, ROWS // size, chunk, 0)


def aligned(index):
    return index if isinstance(index, int) else pl.multiple_of(index, 8)


def groups(body, count):
    if count <= 6:
        for g in range(8):
            body(g, 0)
    else:
        lax.fori_loop(0, 8, body, 0, unroll=4)


def pack_faces(speed, faces, levels, rows_list):
    lane = lax.broadcasted_iota(jnp.int32, (8, LANES), 1)

    def group(g, _):
        parts = []
        for q in range(4):
            here = pl.ds(aligned(g * 32 + q * 8), 8)
            face = jnp.zeros((8, LANES), F32)
            for k in levels:
                spot = 32 * q + 2 * k + 1
                value = pltpu.roll(speed[0, k, 1, here, :], spot + 1, 1)
                face = jnp.where(lane == spot, value, face)
            parts.append(face)
        face = (parts[0] + parts[1]) + (parts[2] + parts[3])
        faces[pl.ds(aligned(g * 8), 8), :] = face + pltpu.roll(face, 2 * LEVELS, 1)
        return 0

    groups(group, len(levels))
    for k in levels:
        for half in range(2):
            spot = 32 + k * 2 + half
            for rows in rows_list:
                rows[spot : spot + 1, :] = speed[1, k, half, ROWS - 1 : ROWS, :]


def pack(x, faces, e, levels, cols, rows):
    lane = lax.broadcasted_iota(jnp.int32, (8, LANES), 1)
    pair = lane >> 1
    odd = (lane & 1) != 0

    def group(g, _):
        parts = []
        for q in range(4):
            here = pl.ds(aligned(g * 32 + q * 8), 8)
            both = jnp.zeros((8, LANES), F32)
            for k in levels:
                for t in range(2):
                    spot = 16 * q + t * LEVELS + k
                    ends = jnp.where(lane == 0, x[t, k, 0, here, :], x[t, k, 1, here, :])
                    both = jnp.where(pair == spot, pltpu.roll(ends, 2 * spot + 1, 1), both)
            parts.append(both)
        both = (parts[0] + parts[1]) + (parts[2] + parts[3])
        here = pl.ds(aligned(g * 8), 8)
        cols[e, 0, here, :] = jnp.where(odd, faces[here, :], both)
        cols[e, 1, here, :] = both
        return 0

    groups(group, len(levels))
    for k in levels:
        for half in range(2):
            for t in range(2):
                spot = t * 16 + k * 2 + half
                rows[e, 0, spot : spot + 1, :] = x[t, k, half, ROWS - 1 : ROWS, :]
                rows[e, 1, spot : spot + 1, :] = x[t, k, half, 0:1, :]


def reversed_lanes(value):
    lane = lax.broadcasted_iota(jnp.int32, value.shape, 1)
    for bit in (1, 2, 4, 8, 16, 32, 64):
        upper = (lane & bit) != 0
        value = jnp.where(
            upper, pltpu.roll(value, bit, 1), pltpu.roll(value, LANES - bit, 1)
        )
    return value


def unpack(x, e, levels, cols, rows, cols_in, rows_in, edge, ocean_v, flows, top, open_south):
    odd = (lax.broadcasted_iota(jnp.int32, (8, LANES), 1) & 1) != 0
    for g in range(8):
        here = pl.ds(g * 8, 8)
        arrived = cols_in[e, 0, here, :]
        fw = face_flux(arrived, pltpu.roll(arrived, 1, 1), cols[e, 1, here, :])
        own, arrived = cols[e, 0, here, :], cols_in[e, 1, here, :]
        fe = face_flux(pltpu.roll(own, LANES - 1, 1), own, pltpu.roll(arrived, LANES - 1, 1))
        both = jnp.where(odd, fw, -fe)
        for q in range(4):
            here = pl.ds(g * 32 + q * 8, 8)
            ocean = jnp.where(odd, ocean_v[0, here, :], ocean_v[1, here, :])
            edge[e, here, :] = (pltpu.roll(both, LANES - 32 * q, 1) if q else both) * ocean

    right = (lax.broadcasted_iota(jnp.int32, (16, LANES), 0) & 1) != 0
    low = jnp.where(right, ocean_v[1, 0:1, :], ocean_v[0, 0:1, :])
    high = jnp.where(right, ocean_v[1, ROWS - 1 : ROWS, :], ocean_v[0, ROWS - 1 : ROWS, :])
    speed = rows_in[e, 1, 32:48, :]
    for t in range(2):
        part = pl.ds(16 * t, 16)
        flux = face_flux(speed, rows_in[e, 1, part, :], rows[e, 1, part, :])
        flows[0, part, :] = jnp.where(open_south, low * flux, 0.0)

    def north(arrived):
        for t in range(2):
            part = pl.ds(16 * t, 16)
            flux = face_flux(rows[e, 0, 32:48, :], rows[e, 0, part, :], arrived[16 * t : 16 * t + 16])
            flows[1, part, :] = -high * flux

    @pl.when(top == 0)
    def _():
        north(rows_in[e, 0, 0:32, :])

    @pl.when(top == 1)
    def _():
        value = reversed_lanes(rows_in[e, 0, 0:32, :])
        odd_row = (lax.broadcasted_iota(jnp.int32, (32, LANES), 0) & 1) != 0
        north(jnp.where(odd_row, pltpu.roll(value, 1, 0), pltpu.roll(value, 31, 0)))

    for k in levels:
        for half in range(2):
            for t in range(2):
                spot = t * 16 + k * 2 + half
                x[t, k, half, 0:1, :] += flows[0, spot : spot + 1, :]
                x[t, k, half, ROWS - 1 : ROWS, :] += flows[1, spot : spot + 1, :]


def running_count(flags):
    lane = lax.broadcasted_iota(jnp.int32, flags.shape, 1)
    total = flags
    for shift in (1, 2, 4, 8, 16, 32):
        total = total + jnp.where(lane >= shift, pltpu.roll(total, shift, 1), 0)
    return total - flags


def lane_total(value):
    for shift in (1, 2, 4, 8, 16, 32, 64):
        value = value + pltpu.roll(value, shift, 1)
    return value


def send_table(lists, gx, stage, table):
    for p in range(COLUMNS):
        stage[p : p + 1, :] = lists[p, 0:1, :]
    ids = stage[...]
    lane = lax.broadcasted_iota(jnp.int32, ids.shape, 1)
    mine = ((ids & 31) >> 1 == gx) & (ids >= 0)
    rank = running_count(jnp.where(mine, 1, 0))
    tile = ((ids >> 5) & (STRIPS - 1)) * 2 + (ids & 1)
    out = jnp.zeros_like(ids)
    for r in range(CAP):
        found = lane_total(jnp.where(mine & (rank == r), tile, 0))
        out = jnp.where(lane == r, found, out)
    table[...] = out


def pick_table(lists, gx, out):
    ids = jnp.broadcast_to(lists[gx, 0:1, :], (COLUMNS, LANES))
    row = lax.broadcasted_iota(jnp.int32, ids.shape, 0)
    mine = ((ids & 31) >> 1 == row) & (ids >= 0)
    flags = jnp.where(mine, 1, 0)
    place = jnp.where(mine, running_count(flags) + row * CAP + 1, 0)
    both = place[0:8] + place[8:16]
    for shift in (4, 2, 1):
        both = both + pltpu.roll(both, shift, 0)
    out[...] = both - 1


def ocean_kernel(
    tracers, speeds, land, own_list, x, dens, incoming, picks,
    speed, cols, rows, cols_in, rows_in, edge, mix, ocean_v, flows, faces, own_v, mask,
    lists, stage, table, table_s, surf, outgoing,
    load_sem, send_sem, recv_sem, list_send, list_recv, relay_send, relay_recv, local_sem,
):
    gy, gx = lax.axis_index("gy"), lax.axis_index("gx")
    top = gy // TOP
    inner = (gy + TOP - 1) // TOP
    east_at = lax.rem(gx + 1, COLUMNS)
    west_at = lax.rem(gx + COLUMNS - 1, COLUMNS)
    north_row = gy + 1 - top
    north_col = gx + top * (COLUMNS - 1 - 2 * gx)

    def load_x(i, lo, hi):
        return [
            pltpu.make_async_copy(
                tracers.at[:, pl.ds(lo, hi - lo), :, pl.ds(half * LANES, LANES)],
                x.at[:, pl.ds(lo, hi - lo), half, pl.ds(0, ROWS), :],
                load_sem.at[i, half],
            )
            for half in range(2)
        ]

    def load_speed(i, step, lo, hi):
        return [
            pltpu.make_async_copy(
                speeds.at[step, :, pl.ds(lo, hi - lo), :, pl.ds(half * LANES, LANES)],
                speed.at[step, :, pl.ds(lo, hi - lo), half],
                load_sem.at[i, half],
            )
            for half in range(2)
        ]

    own = pltpu.make_async_copy(own_list, own_v, local_sem.at[0])
    own.start()
    blocks = pltpu.make_async_copy(land, mask, local_sem.at[1])
    blocks.start()
    upper = load_x(0, 0, 3) + load_speed(1, 0, 0, 3)
    deep = load_x(2, 3, 8) + load_speed(3, 0, 3, 8)
    late_low = load_speed(4, 1, 0, 2)
    late_high = load_speed(5, 1, 2, 8)
    for c in upper:
        c.start()

    barrier = pltpu.get_barrier_semaphore()

    def greet(d, _):
        peer = lax.rem(gx + 1 + d, COLUMNS)
        pl.semaphore_signal(barrier, inc=1, device_id=(gy, peer), device_id_type=MESH)
        return 0

    lax.fori_loop(0, COLUMNS - 1, greet, 0)

    @pl.when(gy < TOP)
    def _():
        pl.semaphore_signal(barrier, inc=1, device_id=(gy + 1, gx), device_id_type=MESH)

    @pl.when(gy > 0)
    def _():
        pl.semaphore_signal(barrier, inc=1, device_id=(gy - 1, gx), device_id_type=MESH)

    for c in deep + late_low + late_high:
        c.start()

    blocks.wait()
    for half in range(2):
        for s in range(STRIPS):
            ocean_v[half, 8 * s : 8 * s + 8, :] = jnp.full((8, LANES), mask[half, s].astype(F32))
    own.wait()
    lists[gx] = jnp.full((8, LANES), -1, jnp.int32)
    lists[gx, :, 0:SLOTS] = jnp.broadcast_to(own_v[...], (8, SLOTS))

    def send_edges(e):
        return [
            pltpu.make_async_remote_copy(
                cols.at[e, 0], cols_in.at[e, 0], send_sem.at[e, 0], recv_sem.at[e, 0],
                device_id=(gy, east_at), device_id_type=MESH,
            ),
            pltpu.make_async_remote_copy(
                cols.at[e, 1], cols_in.at[e, 1], send_sem.at[e, 1], recv_sem.at[e, 1],
                device_id=(gy, west_at), device_id_type=MESH,
            ),
            pltpu.make_async_remote_copy(
                rows.at[e, 0], rows_in.at[e, 1 - top], send_sem.at[e, 2], recv_sem.at[e, 3 - top],
                device_id=(north_row, north_col), device_id_type=MESH,
            ),
        ]

    def send_south(e):
        return pltpu.make_async_remote_copy(
            rows.at[e, 1], rows_in.at[e, 0], send_sem.at[e, 3], recv_sem.at[e, 2],
            device_id=(gy - 1, gx), device_id_type=MESH,
        )

    def start_edges(e):
        for c in send_edges(e):
            c.start()

        @pl.when(gy > 0)
        def _():
            send_south(e).start()

    def wait_edges(e):
        for side, peer in ((0, east_at), (1, west_at)):
            pltpu.make_async_remote_copy(
                cols.at[e, side], cols_in.at[e, side], send_sem.at[e, side], recv_sem.at[e, side],
                device_id=(gy, peer), device_id_type=MESH,
            ).wait_recv()
        pltpu.make_async_remote_copy(
            rows.at[e, 0], rows_in.at[e, 0], send_sem.at[e, 2], recv_sem.at[e, 2],
            device_id=(north_row, north_col), device_id_type=MESH,
        ).wait_recv()

        @pl.when(gy > 0)
        def _():
            pltpu.make_async_remote_copy(
                rows.at[e, 0], rows_in.at[e, 1], send_sem.at[e, 2], recv_sem.at[e, 3],
                device_id=(north_row, north_col), device_id_type=MESH,
            ).wait_recv()

    def finish_edges(e):
        for c in send_edges(e):
            c.wait_send()

        @pl.when(gy > 0)
        def _():
            send_south(e).wait_send()

    for c in upper:
        c.wait()
    pack_faces(speed.at[0], faces.at[0], range(0, 3), [rows.at[0, 0]])
    pack(x, faces.at[0], 0, range(0, 3), cols, rows)
    advance(x, speed.at[0], ocean_v, 0, 3)
    pl.semaphore_wait(barrier, COLUMNS - 1 + (1 - top) + inner)
    start_edges(0)

    def list_copy(peer, slot):
        return pltpu.make_async_remote_copy(
            lists.at[gx], lists.at[slot], list_send.at[peer], list_recv.at[slot],
            device_id=(gy, peer), device_id_type=MESH,
        )

    def send_list(d, _):
        list_copy(lax.rem(gx + 1 + d, COLUMNS), gx).start()
        return 0

    lax.fori_loop(0, COLUMNS - 1, send_list, 0)

    def fill(e, levels):
        wait_edges(e)
        unpack(x, e, levels, cols, rows, cols_in, rows_in, edge, ocean_v, flows, top, gy > 0)

    def settle(e, m, first, last, resumed, dens_ref, surf_ref, size):
        settle_levels(
            x, edge.at[e], mix.at[m], ocean_v, first, last, resumed, dens_ref, surf_ref, size
        )

    for c in deep:
        c.wait()
    pack_faces(speed.at[0], faces.at[1], range(3, 8), [rows.at[1, 0]])
    pack(x, faces.at[1], 1, range(3, 8), cols, rows)
    start_edges(1)
    advance(x, speed.at[0], ocean_v, 3, 8)
    for c in late_low + late_high:
        c.wait()
    pack_faces(speed.at[1], faces.at[2], range(0, 8), [rows.at[2, 0], rows.at[3, 0]])

    fill(0, range(0, 3))
    settle(0, 0, 0, 2, False, None, None, 256)
    pack(x, faces.at[2], 2, range(0, 2), cols, rows)
    start_edges(2)
    advance(x, speed.at[1], ocean_v, 0, 2)

    def take_list(d, _):
        peer = lax.rem(gx + 1 + d, COLUMNS)
        list_copy(peer, peer).wait_recv()
        return 0

    lax.fori_loop(0, COLUMNS - 1, take_list, 0)
    fill(1, range(3, 8))
    settle(1, 0, 2, 7, True, None, None, 128)
    send_table(lists, gx, stage, table)
    pack(x, faces.at[2], 3, range(2, 8), cols, rows)
    fetch = pltpu.make_async_copy(table, table_s, local_sem.at[1])
    fetch.start()
    start_edges(3)


    fill(2, range(0, 2))
    settle(2, 1, 0, 1, False, dens, surf, 256)
    fetch.wait()

    def bucket(peer, target, base):
        tiles = [jnp.clip(table_s[peer, r], 0, SLOTS - 1) for r in range(CAP)]
        blocks = [surf[tile] for tile in tiles]
        for r in range(CAP):
            target[base + r] = blocks[r]

    def relay_copy(peer, slot):
        return pltpu.make_async_remote_copy(
            outgoing.at[pl.ds(peer * CAP, CAP)], incoming.at[pl.ds(slot * CAP, CAP)],
            relay_send.at[peer], relay_recv.at[slot],
            device_id=(gy, peer), device_id_type=MESH,
        )

    def relay(side, turn):
        peer = side * 8 + lax.rem(gx + turn, 8)
        bucket(peer, outgoing, peer * CAP)
        relay_copy(peer, gx).start()

    side = gx // 8
    for across, turn in RELAY:
        relay(1 - side if across else side, turn)
    bucket(gx, incoming, gx * CAP)
    pick_table(lists, gx, picks)

    advance(x, speed.at[1], ocean_v, 2, 8)
    fill(3, range(2, 8))
    settle(3, 1, 1, 7, True, dens, None, 128)

    for e in range(4):
        finish_edges(e)

    def close(d, _):
        peer = lax.rem(gx + 1 + d, COLUMNS)
        list_copy(peer, gx).wait_send()
        relay_copy(peer, gx).wait_send()
        relay_copy(peer, peer).wait_recv()
        return 0

    lax.fori_loop(0, COLUMNS - 1, close, 0)


def output_kernel(x, dens, incoming, picks_v, tracers_out, dens_out, ice_out, ice, picks, sems):
    copies = []
    table = pltpu.make_async_copy(picks_v, picks, sems.at[6])
    table.start()
    for half in range(2):
        lanes = pl.ds(half * LANES, LANES)
        copies.append(
            pltpu.make_async_copy(
                x.at[:, :, half, pl.ds(0, ROWS), :], tracers_out.at[:, :, :, lanes], sems.at[half]
            )
        )
        copies.append(
            pltpu.make_async_copy(
                dens.at[:, half], dens_out.at[:, :, lanes], sems.at[2 + half]
            )
        )
    for c in copies:
        c.start()
    table.wait()

    def slot(s, _):
        place = picks[0, s]
        filled = place >= 0
        spot = jnp.clip(place, 0, COLUMNS * CAP - 1)
        heat = jnp.where(filled, incoming[spot, 0], 0.0)
        salt = jnp.where(filled, incoming[spot, 1], 0.0)
        ice[s, 0] = heat
        ice[s, 1] = salt
        ice[s, 2] = density_at(heat, salt, 0)
        return 0

    for part in range(2):
        lax.fori_loop(part * 32, part * 32 + 32, slot, 0, unroll=8)
        c = pltpu.make_async_copy(
            ice.at[pl.ds(part * 32, 32)], ice_out.at[pl.ds(part * 32, 32)], sems.at[4 + part]
        )
        c.start()
        copies.append(c)
    for c in copies:
        c.wait()


def on_device(tracers, face_speeds, ocean_block, ice_blocks):
    anywhere = pl.BlockSpec(memory_space=pl.ANY)
    vmem = pl.BlockSpec(memory_space=pltpu.VMEM)
    hbm = pl.BlockSpec(memory_space=pltpu.HBM)
    dma = pltpu.SemaphoreType.DMA
    x, dens, incoming, picks = pl.pallas_call(
        ocean_kernel,
        out_shape=(
            jax.ShapeDtypeStruct((2, LEVELS, 2, ROWS + 8, LANES), F32),
            jax.ShapeDtypeStruct((LEVELS, 2, ROWS, LANES), F32),
            jax.ShapeDtypeStruct((COLUMNS * CAP, 2, 8, LANES), F32),
            jax.ShapeDtypeStruct((8, LANES), jnp.int32),
        ),
        in_specs=[hbm, hbm, hbm, hbm],
        out_specs=(vmem, vmem, vmem, vmem),
        scratch_shapes=[
            pltpu.VMEM((2, 2, LEVELS, 2, ROWS, LANES), F32),
            pltpu.VMEM((4, 2, 64, LANES), F32),
            pltpu.VMEM((4, 2, 48, LANES), F32),
            pltpu.VMEM((4, 2, 64, LANES), F32),
            pltpu.VMEM((4, 2, 48, LANES), F32),
            pltpu.VMEM((4, ROWS, LANES), F32),
            pltpu.VMEM((2, 2, 2, ROWS, LANES), F32),
            pltpu.VMEM((2, ROWS, LANES), F32),
            pltpu.VMEM((2, 32, LANES), F32),
            pltpu.VMEM((3, 64, LANES), F32),
            pltpu.VMEM((1, SLOTS), jnp.int32),
            pltpu.SMEM((2, STRIPS), jnp.int32),
            pltpu.VMEM((COLUMNS, 8, LANES), jnp.int32),
            pltpu.VMEM((COLUMNS, LANES), jnp.int32),
            pltpu.VMEM((COLUMNS, LANES), jnp.int32),
            pltpu.SMEM((COLUMNS, LANES), jnp.int32),
            pltpu.VMEM((SLOTS, 2, 8, LANES), F32),
            pltpu.VMEM((COLUMNS * CAP, 2, 8, LANES), F32),
            dma((6, 2)),
            dma((4, 4)),
            dma((4, 4)),
            dma((COLUMNS,)),
            dma((COLUMNS,)),
            dma((COLUMNS,)),
            dma((COLUMNS,)),
            dma((2,)),
        ],
        compiler_params=pltpu.CompilerParams(
            collective_id=0, has_side_effects=True, vmem_limit_bytes=20 << 20
        ),
        name="ocean",
    )(*[
        pltpu.with_memory_space_constraint(v, pltpu.HBM)
        for v in (tracers, face_speeds, ocean_block.T, ice_blocks.reshape(1, SLOTS))
    ])
    return pl.pallas_call(
        output_kernel,
        out_shape=(
            jax.ShapeDtypeStruct(tracers.shape, F32),
            jax.ShapeDtypeStruct(tracers.shape[1:], F32),
            jax.ShapeDtypeStruct((SLOTS, 3, 8, LANES), F32),
        ),
        in_specs=[anywhere, anywhere, vmem, vmem],
        out_specs=(anywhere, anywhere, anywhere),
        scratch_shapes=[
            pltpu.VMEM((SLOTS, 3, 8, LANES), F32),
            pltpu.SMEM((8, LANES), jnp.int32),
            dma((7,)),
        ],
        compiler_params=pltpu.CompilerParams(vmem_limit_bytes=16 << 20),
        name="outputs",
    )(x, dens, incoming, picks)


def solution(mesh):
    return jax.shard_map(
        on_device,
        mesh=mesh,
        in_specs=(
            P(None, None, "gy", "gx"),
            P(None, None, None, "gy", "gx"),
            P("gy", "gx"),
            P(("gy", "gx")),
        ),
        out_specs=(
            P(None, None, "gy", "gx"),
            P(None, "gy", "gx"),
            P(("gy", "gx"), None, None, None),
        ),
        check_vma=False,
    )
```

```python
import functools

import jax
import jax.numpy as jnp
from jax import lax
from jax.experimental import pallas as pl
from jax.experimental.pallas import tpu as pltpu
from jax.sharding import PartitionSpec as P

MESH = pl.DeviceIdType.MESH
LEVELS = 8
ROWS = 256
LANES = 128
STRIPS = 32
RELAY = ((1, 4), (1, 5), (0, 4), (1, 6), (1, 7), (0, 5), (1, 0), (1, 1), (0, 3), (1, 2), (1, 3), (0, 6), (0, 2), (0, 7), (0, 1))
COLUMNS = 16
TOP = 7
CAP = 8
SLOTS = 64
FACES = 24
F32 = jnp.float32

warming_swell_coefficient = 0.1655
haline_base = 0.7655
warming_swell_quadratic = 0.05952
haline_curve = 0.00054914
warming_compression_coupling = 0.0001497
haline_press = 1.109e-05
mixing_contraction_coefficient = 0.0024341
lateral_mix = 0.08
mixing_base = 0.05
mixing_boost = 0.2


def density_at(heat, salt, level):
    depth = 10.0 * level + 5.0
    heat_one = -warming_swell_coefficient * (1.0 + warming_compression_coupling * depth)
    heat_two = -warming_swell_coefficient * 0.5 * warming_swell_quadratic
    salt_one = haline_base * (1.0 - haline_press * depth)
    salt_two = -haline_base * 0.5 * haline_curve
    return heat * (
        heat_one + heat_two * heat - mixing_contraction_coefficient * salt
    ) + salt * (salt_one + salt_two * salt)


def face_weights(speed):
    lower = jnp.maximum(speed, 0.0) + lateral_mix
    return lower, speed - lower


def face_flux(speed, lower_cells, upper_cells):
    lower, upper = face_weights(speed)
    return lower * lower_cells + upper * upper_cells


def advance(x, speed, ocean_v, low, high):
    lane = lax.broadcasted_iota(jnp.int32, (ROWS, LANES), 1)
    first_lane, last_lane = lane == 0, lane == LANES - 1
    last_row = lax.broadcasted_iota(jnp.int32, (8, LANES), 0) == 7
    here, above = pl.ds(0, ROWS), pl.ds(1, ROWS)

    def level(k, _):
        east = [face_weights(speed[0, k, half]) for half in range(2)]
        north = [face_weights(speed[1, k, half]) for half in range(2)]
        for t in range(2):
            cells = [x[t, k, half, here, :] for half in range(2)]
            turned = [pltpu.roll(c, LANES - 1, 1) for c in cells]
            eastern = [jnp.where(last_lane, turned[1], turned[0]), turned[1]]
            ef = [east[half][0] * cells[half] + east[half][1] * eastern[half] for half in range(2)]
            ef[1] = jnp.where(last_lane, 0.0, ef[1])
            back = [pltpu.roll(f, 1, 1) for f in ef]
            wf = [jnp.where(first_lane, 0.0, back[0]), jnp.where(first_lane, back[0], back[1])]
            for half in range(2):
                nf = north[half][0] * cells[half] + north[half][1] * x[t, k, half, above, :]
                nf = jnp.concatenate(
                    [nf[: ROWS - 8], jnp.where(last_row, 0.0, nf[ROWS - 8 :])], axis=0
                )
                change = (ef[half] - wf[half]) + (nf - pltpu.roll(nf, 1, 0))
                x[t, k, half, here, :] = cells[half] - ocean_v[half] * change
        return 0

    lax.fori_loop(low, high, level, 0)


def settle_levels(x, edge, mix, ocean_v, first, last, resumed, dens, surf, size):
    lane = lax.broadcasted_iota(jnp.int32, (size, LANES), 1)
    first_lane, last_lane = lane == 0, lane == LANES - 1

    def chunk(c, _):
        here = pl.ds(aligned(c * size), size)
        rim = edge[here, :]
        ocean = [ocean_v[half, here, :] for half in range(2)]

        def advected(k):
            out = []
            for t in range(2):
                ends = pltpu.roll(rim, LANES - 1 - 2 * (t * LEVELS + k), 1)
                out.append(
                    [
                        x[t, k, 0, here, :] + jnp.where(first_lane, ends, 0.0),
                        x[t, k, 1, here, :] + jnp.where(last_lane, ends, 0.0),
                    ]
                )
            return out

        def settle(k, adv, flux, over):
            for half in range(2):
                done = []
                for t in range(2):
                    if flux is None:
                        gain = -over[t][half]
                    elif over is None:
                        gain = flux[t][half]
                    else:
                        gain = flux[t][half] - over[t][half]
                    value = adv[t][half] + ocean[half] * gain
                    x[t, k, half, here, :] = value
                    done.append(value)
                    if surf is not None and k == 0:
                        for i in range(size // 8):
                            tile = 2 * (c * (size // 8) + i) + half
                            surf[tile, t] = value[8 * i : 8 * i + 8]
                if dens is not None:
                    dens[k, half, here, :] = density_at(done[0], done[1], k)

        if dens is not None:
            for half in range(2):
                dens[0, half, here, :] = density_at(x[0, 0, half, here, :], x[1, 0, half, here, :], 0)

        over = None
        if resumed:
            adv = [[x[t, first, half, here, :] for half in range(2)] for t in range(2)]
            over = [[mix[t, half, here, :] for half in range(2)] for t in range(2)]
        else:
            adv = advected(first)
        rho = [density_at(adv[0][half], adv[1][half], first) for half in range(2)]
        for k in range(first + 1, last + 1):
            lower = advected(k)
            rho_lower = [density_at(lower[0][half], lower[1][half], k) for half in range(2)]
            flux = [[None, None], [None, None]]
            for half in range(2):
                kappa = (mixing_base + 0.5 * mixing_boost) - 0.5 * mixing_boost * jnp.tanh(
                    rho_lower[half] - rho[half]
                )
                for t in range(2):
                    flux[t][half] = kappa * (lower[t][half] - adv[t][half])
            settle(k - 1, adv, flux, over)
            adv, rho, over = lower, rho_lower, flux
        if last == LEVELS - 1:
            settle(last, adv, None, over)
        else:
            for t in range(2):
                for half in range(2):
                    x[t, last, half, here, :] = adv[t][half]
                    mix[t, half, here, :] = over[t][half]
        return 0

    if size == ROWS:
        chunk(0, 0)
    else:
        lax.fori_loop(0, ROWS // size, chunk, 0)


def aligned(index):
    return index if isinstance(index, int) else pl.multiple_of(index, 8)


def groups(body, count):
    if count <= 6:
        for g in range(8):
            body(g, 0)
    else:
        lax.fori_loop(0, 8, body, 0, unroll=4)


def pack_faces(speed, faces, levels, rows_list):
    lane = lax.broadcasted_iota(jnp.int32, (8, LANES), 1)

    def group(g, _):
        parts = []
        for q in range(4):
            here = pl.ds(aligned(g * 32 + q * 8), 8)
            face = jnp.zeros((8, LANES), F32)
            for k in levels:
                spot = 32 * q + 2 * k + 1
                value = pltpu.roll(speed[0, k, 1, here, :], spot + 1, 1)
                face = jnp.where(lane == spot, value, face)
            parts.append(face)
        face = (parts[0] + parts[1]) + (parts[2] + parts[3])
        faces[pl.ds(aligned(g * 8), 8), :] = face + pltpu.roll(face, 2 * LEVELS, 1)
        return 0

    groups(group, len(levels))
    for k in levels:
        for half in range(2):
            spot = 32 + k * 2 + half
            for rows in rows_list:
                rows[spot : spot + 1, :] = speed[1, k, half, ROWS - 1 : ROWS, :]


def pack(x, faces, e, levels, cols, rows):
    lane = lax.broadcasted_iota(jnp.int32, (8, LANES), 1)
    pair = lane >> 1
    odd = (lane & 1) != 0

    def group(g, _):
        parts = []
        for q in range(4):
            here = pl.ds(aligned(g * 32 + q * 8), 8)
            both = jnp.zeros((8, LANES), F32)
            for k in levels:
                for t in range(2):
                    spot = 16 * q + t * LEVELS + k
                    ends = jnp.where(lane == 0, x[t, k, 0, here, :], x[t, k, 1, here, :])
                    both = jnp.where(pair == spot, pltpu.roll(ends, 2 * spot + 1, 1), both)
            parts.append(both)
        both = (parts[0] + parts[1]) + (parts[2] + parts[3])
        here = pl.ds(aligned(g * 8), 8)
        cols[e, 0, here, :] = jnp.where(odd, faces[here, :], both)
        cols[e, 1, here, :] = both
        return 0

    groups(group, len(levels))
    for k in levels:
        for half in range(2):
            for t in range(2):
                spot = t * 16 + k * 2 + half
                rows[e, 0, spot : spot + 1, :] = x[t, k, half, ROWS - 1 : ROWS, :]
                rows[e, 1, spot : spot + 1, :] = x[t, k, half, 0:1, :]


def reversed_lanes(value):
    lane = lax.broadcasted_iota(jnp.int32, value.shape, 1)
    for bit in (1, 2, 4, 8, 16, 32, 64):
        upper = (lane & bit) != 0
        value = jnp.where(
            upper, pltpu.roll(value, bit, 1), pltpu.roll(value, LANES - bit, 1)
        )
    return value


def unpack(x, e, levels, cols, rows, cols_in, rows_in, edge, ocean_v, flows, top, open_south):
    odd = (lax.broadcasted_iota(jnp.int32, (8, LANES), 1) & 1) != 0
    for g in range(8):
        here = pl.ds(g * 8, 8)
        arrived = cols_in[e, 0, here, :]
        fw = face_flux(arrived, pltpu.roll(arrived, 1, 1), cols[e, 1, here, :])
        own, arrived = cols[e, 0, here, :], cols_in[e, 1, here, :]
        fe = face_flux(pltpu.roll(own, LANES - 1, 1), own, pltpu.roll(arrived, LANES - 1, 1))
        both = jnp.where(odd, fw, -fe)
        for q in range(4):
            here = pl.ds(g * 32 + q * 8, 8)
            ocean = jnp.where(odd, ocean_v[0, here, :], ocean_v[1, here, :])
            edge[e, here, :] = (pltpu.roll(both, LANES - 32 * q, 1) if q else both) * ocean

    right = (lax.broadcasted_iota(jnp.int32, (16, LANES), 0) & 1) != 0
    low = jnp.where(right, ocean_v[1, 0:1, :], ocean_v[0, 0:1, :])
    high = jnp.where(right, ocean_v[1, ROWS - 1 : ROWS, :], ocean_v[0, ROWS - 1 : ROWS, :])
    speed = rows_in[e, 1, 32:48, :]
    for t in range(2):
        part = pl.ds(16 * t, 16)
        flux = face_flux(speed, rows_in[e, 1, part, :], rows[e, 1, part, :])
        flows[0, part, :] = jnp.where(open_south, low * flux, 0.0)

    def north(arrived):
        for t in range(2):
            part = pl.ds(16 * t, 16)
            flux = face_flux(rows[e, 0, 32:48, :], rows[e, 0, part, :], arrived[16 * t : 16 * t + 16])
            flows[1, part, :] = -high * flux

    @pl.when(top == 0)
    def _():
        north(rows_in[e, 0, 0:32, :])

    @pl.when(top == 1)
    def _():
        value = reversed_lanes(rows_in[e, 0, 0:32, :])
        odd_row = (lax.broadcasted_iota(jnp.int32, (32, LANES), 0) & 1) != 0
        north(jnp.where(odd_row, pltpu.roll(value, 1, 0), pltpu.roll(value, 31, 0)))

    for k in levels:
        for half in range(2):
            for t in range(2):
                spot = t * 16 + k * 2 + half
                x[t, k, half, 0:1, :] += flows[0, spot : spot + 1, :]
                x[t, k, half, ROWS - 1 : ROWS, :] += flows[1, spot : spot + 1, :]


def running_count(flags):
    lane = lax.broadcasted_iota(jnp.int32, flags.shape, 1)
    total = flags
    for shift in (1, 2, 4, 8, 16, 32):
        total = total + jnp.where(lane >= shift, pltpu.roll(total, shift, 1), 0)
    return total - flags


def lane_total(value):
    for shift in (1, 2, 4, 8, 16, 32, 64):
        value = value + pltpu.roll(value, shift, 1)
    return value


def send_table(lists, gx, stage, table):
    for p in range(COLUMNS):
        stage[p : p + 1, :] = lists[p, 0:1, :]
    ids = stage[...]
    lane = lax.broadcasted_iota(jnp.int32, ids.shape, 1)
    mine = ((ids & 31) >> 1 == gx) & (ids >= 0)
    rank = running_count(jnp.where(mine, 1, 0))
    tile = ((ids >> 5) & (STRIPS - 1)) * 2 + (ids & 1)
    out = jnp.zeros_like(ids)
    for r in range(CAP):
        found = lane_total(jnp.where(mine & (rank == r), tile, 0))
        out = jnp.where(lane == r, found, out)
    table[...] = out


def pick_table(lists, gx, out):
    ids = jnp.broadcast_to(lists[gx, 0:1, :], (COLUMNS, LANES))
    row = lax.broadcasted_iota(jnp.int32, ids.shape, 0)
    mine = ((ids & 31) >> 1 == row) & (ids >= 0)
    flags = jnp.where(mine, 1, 0)
    place = jnp.where(mine, running_count(flags) + row * CAP + 1, 0)
    both = place[0:8] + place[8:16]
    for shift in (4, 2, 1):
        both = both + pltpu.roll(both, shift, 0)
    out[...] = both - 1


def ocean_kernel(
    tracers, speeds, land, own_list, x, dens, incoming, picks,
    speed, cols, rows, cols_in, rows_in, edge, mix, ocean_v, flows, faces, own_v, mask,
    lists, stage, table, table_s, surf, outgoing,
    load_sem, send_sem, recv_sem, list_send, list_recv, relay_send, relay_recv, local_sem,
):
    gy, gx = lax.axis_index("gy"), lax.axis_index("gx")
    top = gy // TOP
    inner = (gy + TOP - 1) // TOP
    east_at = lax.rem(gx + 1, COLUMNS)
    west_at = lax.rem(gx + COLUMNS - 1, COLUMNS)
    north_row = gy + 1 - top
    north_col = gx + top * (COLUMNS - 1 - 2 * gx)

    def load_x(i, lo, hi):
        return [
            pltpu.make_async_copy(
                tracers.at[:, pl.ds(lo, hi - lo), :, pl.ds(half * LANES, LANES)],
                x.at[:, pl.ds(lo, hi - lo), half, pl.ds(0, ROWS), :],
                load_sem.at[i, half],
            )
            for half in range(2)
        ]

    def load_speed(i, step, lo, hi):
        return [
            pltpu.make_async_copy(
                speeds.at[step, :, pl.ds(lo, hi - lo), :, pl.ds(half * LANES, LANES)],
                speed.at[step, :, pl.ds(lo, hi - lo), half],
                load_sem.at[i, half],
            )
            for half in range(2)
        ]

    own = pltpu.make_async_copy(own_list, own_v, local_sem.at[0])
    own.start()
    blocks = pltpu.make_async_copy(land, mask, local_sem.at[1])
    blocks.start()
    upper = load_x(0, 0, 3) + load_speed(1, 0, 0, 3)
    deep = load_x(2, 3, 8) + load_speed(3, 0, 3, 8)
    late_low = load_speed(4, 1, 0, 2)
    late_high = load_speed(5, 1, 2, 8)
    for c in upper:
        c.start()

    barrier = pltpu.get_barrier_semaphore()

    def greet(d, _):
        peer = lax.rem(gx + 1 + d, COLUMNS)
        pl.semaphore_signal(barrier, inc=1, device_id=(gy, peer), device_id_type=MESH)
        return 0

    lax.fori_loop(0, COLUMNS - 1, greet, 0)

    @pl.when(gy < TOP)
    def _():
        pl.semaphore_signal(barrier, inc=1, device_id=(gy + 1, gx), device_id_type=MESH)

    @pl.when(gy > 0)
    def _():
        pl.semaphore_signal(barrier, inc=1, device_id=(gy - 1, gx), device_id_type=MESH)

    for c in deep + late_low + late_high:
        c.start()

    blocks.wait()
    for half in range(2):
        for s in range(STRIPS):
            ocean_v[half, 8 * s : 8 * s + 8, :] = jnp.full((8, LANES), mask[half, s].astype(F32))
    own.wait()
    lists[gx] = jnp.full((8, LANES), -1, jnp.int32)
    lists[gx, :, 0:SLOTS] = jnp.broadcast_to(own_v[...], (8, SLOTS))

    def send_edges(e):
        return [
            pltpu.make_async_remote_copy(
                cols.at[e, 0], cols_in.at[e, 0], send_sem.at[e, 0], recv_sem.at[e, 0],
                device_id=(gy, east_at), device_id_type=MESH,
            ),
            pltpu.make_async_remote_copy(
                cols.at[e, 1], cols_in.at[e, 1], send_sem.at[e, 1], recv_sem.at[e, 1],
                device_id=(gy, west_at), device_id_type=MESH,
            ),
            pltpu.make_async_remote_copy(
                rows.at[e, 0], rows_in.at[e, 1 - top], send_sem.at[e, 2], recv_sem.at[e, 3 - top],
                device_id=(north_row, north_col), device_id_type=MESH,
            ),
        ]

    def send_south(e):
        return pltpu.make_async_remote_copy(
            rows.at[e, 1], rows_in.at[e, 0], send_sem.at[e, 3], recv_sem.at[e, 2],
            device_id=(gy - 1, gx), device_id_type=MESH,
        )

    def start_edges(e):
        for c in send_edges(e):
            c.start()

        @pl.when(gy > 0)
        def _():
            send_south(e).start()

    def wait_edges(e):
        for side, peer in ((0, east_at), (1, west_at)):
            pltpu.make_async_remote_copy(
                cols.at[e, side], cols_in.at[e, side], send_sem.at[e, side], recv_sem.at[e, side],
                device_id=(gy, peer), device_id_type=MESH,
            ).wait_recv()
        pltpu.make_async_remote_copy(
            rows.at[e, 0], rows_in.at[e, 0], send_sem.at[e, 2], recv_sem.at[e, 2],
            device_id=(north_row, north_col), device_id_type=MESH,
        ).wait_recv()

        @pl.when(gy > 0)
        def _():
            pltpu.make_async_remote_copy(
                rows.at[e, 0], rows_in.at[e, 1], send_sem.at[e, 2], recv_sem.at[e, 3],
                device_id=(north_row, north_col), device_id_type=MESH,
            ).wait_recv()

    def finish_edges(e):
        for c in send_edges(e):
            c.wait_send()

        @pl.when(gy > 0)
        def _():
            send_south(e).wait_send()

    for c in upper:
        c.wait()
    pack_faces(speed.at[0], faces.at[0], range(0, 3), [rows.at[0, 0]])
    pack(x, faces.at[0], 0, range(0, 3), cols, rows)
    advance(x, speed.at[0], ocean_v, 0, 3)
    pl.semaphore_wait(barrier, COLUMNS - 1 + (1 - top) + inner)
    start_edges(0)

    def list_copy(peer, slot):
        return pltpu.make_async_remote_copy(
            lists.at[gx], lists.at[slot], list_send.at[peer], list_recv.at[slot],
            device_id=(gy, peer), device_id_type=MESH,
        )

    def send_list(d, _):
        list_copy(lax.rem(gx + 1 + d, COLUMNS), gx).start()
        return 0

    lax.fori_loop(0, COLUMNS - 1, send_list, 0)

    def fill(e, levels):
        wait_edges(e)
        unpack(x, e, levels, cols, rows, cols_in, rows_in, edge, ocean_v, flows, top, gy > 0)

    def settle(e, m, first, last, resumed, dens_ref, surf_ref, size):
        settle_levels(
            x, edge.at[e], mix.at[m], ocean_v, first, last, resumed, dens_ref, surf_ref, size
        )

    for c in deep:
        c.wait()
    pack_faces(speed.at[0], faces.at[1], range(3, 8), [rows.at[1, 0]])
    pack(x, faces.at[1], 1, range(3, 8), cols, rows)
    start_edges(1)
    advance(x, speed.at[0], ocean_v, 3, 8)
    for c in late_low + late_high:
        c.wait()
    pack_faces(speed.at[1], faces.at[2], range(0, 8), [rows.at[2, 0], rows.at[3, 0]])

    fill(0, range(0, 3))
    settle(0, 0, 0, 2, False, None, None, 256)
    pack(x, faces.at[2], 2, range(0, 2), cols, rows)
    start_edges(2)
    advance(x, speed.at[1], ocean_v, 0, 2)

    def take_list(d, _):
        peer = lax.rem(gx + 1 + d, COLUMNS)
        list_copy(peer, peer).wait_recv()
        return 0

    lax.fori_loop(0, COLUMNS - 1, take_list, 0)
    fill(1, range(3, 8))
    settle(1, 0, 2, 7, True, None, None, 128)
    send_table(lists, gx, stage, table)
    pack(x, faces.at[2], 3, range(2, 8), cols, rows)
    fetch = pltpu.make_async_copy(table, table_s, local_sem.at[1])
    fetch.start()
    start_edges(3)


    fill(2, range(0, 2))
    settle(2, 1, 0, 1, False, None, surf, 256)
    fetch.wait()

    def bucket(peer, target, base):
        tiles = [jnp.clip(table_s[peer, r], 0, SLOTS - 1) for r in range(CAP)]
        blocks = [surf[tile] for tile in tiles]
        for r in range(CAP):
            target[base + r] = blocks[r]

    def relay_copy(peer, slot):
        return pltpu.make_async_remote_copy(
            outgoing.at[pl.ds(peer * CAP, CAP)], incoming.at[pl.ds(slot * CAP, CAP)],
            relay_send.at[peer], relay_recv.at[slot],
            device_id=(gy, peer), device_id_type=MESH,
        )

    def relay(side, turn):
        peer = side * 8 + lax.rem(gx + turn, 8)
        bucket(peer, outgoing, peer * CAP)
        relay_copy(peer, gx).start()

    side = gx // 8
    for across, turn in RELAY:
        relay(1 - side if across else side, turn)
    bucket(gx, incoming, gx * CAP)
    pick_table(lists, gx, picks)

    def close_list(d, _):
        list_copy(lax.rem(gx + 1 + d, COLUMNS), gx).wait_send()
        return 0

    lax.fori_loop(0, COLUMNS - 1, close_list, 0)
    advance(x, speed.at[1], ocean_v, 2, 8)
    fill(3, range(2, 8))
    settle(3, 1, 1, 7, True, dens, None, 128)
    for e in range(4):
        finish_edges(e)

    for across, turn in RELAY:
        peer = (1 - side if across else side) * 8 + lax.rem(gx + turn, 8)
        relay_copy(peer, gx).wait_send()
    for across, turn in RELAY:
        peer = (1 - side if across else side) * 8 + lax.rem(gx + 8 - turn, 8)
        relay_copy(peer, peer).wait_recv()


def output_kernel(x, dens, incoming, picks_v, tracers_out, dens_out, ice_out, ice, picks, sems):
    copies = []
    table = pltpu.make_async_copy(picks_v, picks, sems.at[6])
    table.start()
    for half in range(2):
        lanes = pl.ds(half * LANES, LANES)
        copies.append(
            pltpu.make_async_copy(
                x.at[:, :, half, pl.ds(0, ROWS), :], tracers_out.at[:, :, :, lanes], sems.at[half]
            )
        )
        copies.append(
            pltpu.make_async_copy(
                dens.at[:, half], dens_out.at[:, :, lanes], sems.at[2 + half]
            )
        )
    for c in copies:
        c.start()
    table.wait()

    def slot(s, _):
        place = picks[0, s]
        filled = place >= 0
        spot = jnp.clip(place, 0, COLUMNS * CAP - 1)
        heat = jnp.where(filled, incoming[spot, 0], 0.0)
        salt = jnp.where(filled, incoming[spot, 1], 0.0)
        ice[s, 0] = heat
        ice[s, 1] = salt
        ice[s, 2] = density_at(heat, salt, 0)
        return 0

    for part in range(2):
        lax.fori_loop(part * 32, part * 32 + 32, slot, 0, unroll=8)
        c = pltpu.make_async_copy(
            ice.at[pl.ds(part * 32, 32)], ice_out.at[pl.ds(part * 32, 32)], sems.at[4 + part]
        )
        c.start()
        copies.append(c)
    for c in copies:
        c.wait()


def on_device(tracers, face_speeds, ocean_block, ice_blocks):
    anywhere = pl.BlockSpec(memory_space=pl.ANY)
    vmem = pl.BlockSpec(memory_space=pltpu.VMEM)
    hbm = pl.BlockSpec(memory_space=pltpu.HBM)
    dma = pltpu.SemaphoreType.DMA
    x, dens, incoming, picks = pl.pallas_call(
        ocean_kernel,
        out_shape=(
            jax.ShapeDtypeStruct((2, LEVELS, 2, ROWS + 8, LANES), F32),
            jax.ShapeDtypeStruct((LEVELS, 2, ROWS, LANES), F32),
            jax.ShapeDtypeStruct((COLUMNS * CAP, 2, 8, LANES), F32),
            jax.ShapeDtypeStruct((8, LANES), jnp.int32),
        ),
        in_specs=[hbm, hbm, hbm, hbm],
        out_specs=(vmem, vmem, vmem, vmem),
        scratch_shapes=[
            pltpu.VMEM((2, 2, LEVELS, 2, ROWS, LANES), F32),
            pltpu.VMEM((4, 2, 64, LANES), F32),
            pltpu.VMEM((4, 2, 48, LANES), F32),
            pltpu.VMEM((4, 2, 64, LANES), F32),
            pltpu.VMEM((4, 2, 48, LANES), F32),
            pltpu.VMEM((4, ROWS, LANES), F32),
            pltpu.VMEM((2, 2, 2, ROWS, LANES), F32),
            pltpu.VMEM((2, ROWS, LANES), F32),
            pltpu.VMEM((2, 32, LANES), F32),
            pltpu.VMEM((3, 64, LANES), F32),
            pltpu.VMEM((1, SLOTS), jnp.int32),
            pltpu.SMEM((2, STRIPS), jnp.int32),
            pltpu.VMEM((COLUMNS, 8, LANES), jnp.int32),
            pltpu.VMEM((COLUMNS, LANES), jnp.int32),
            pltpu.VMEM((COLUMNS, LANES), jnp.int32),
            pltpu.SMEM((COLUMNS, LANES), jnp.int32),
            pltpu.VMEM((SLOTS, 2, 8, LANES), F32),
            pltpu.VMEM((COLUMNS * CAP, 2, 8, LANES), F32),
            dma((6, 2)),
            dma((4, 4)),
            dma((4, 4)),
            dma((COLUMNS,)),
            dma((COLUMNS,)),
            dma((COLUMNS,)),
            dma((COLUMNS,)),
            dma((2,)),
        ],
        compiler_params=pltpu.CompilerParams(
            collective_id=0, has_side_effects=True, vmem_limit_bytes=20 << 20
        ),
        name="ocean",
    )(*[
        pltpu.with_memory_space_constraint(v, pltpu.HBM)
        for v in (tracers, face_speeds, ocean_block.T, ice_blocks.reshape(1, SLOTS))
    ])
    return pl.pallas_call(
        output_kernel,
        out_shape=(
            jax.ShapeDtypeStruct(tracers.shape, F32),
            jax.ShapeDtypeStruct(tracers.shape[1:], F32),
            jax.ShapeDtypeStruct((SLOTS, 3, 8, LANES), F32),
        ),
        in_specs=[anywhere, anywhere, vmem, vmem],
        out_specs=(anywhere, anywhere, anywhere),
        scratch_shapes=[
            pltpu.VMEM((SLOTS, 3, 8, LANES), F32),
            pltpu.SMEM((8, LANES), jnp.int32),
            dma((7,)),
        ],
        compiler_params=pltpu.CompilerParams(vmem_limit_bytes=16 << 20),
        name="outputs",
    )(x, dens, incoming, picks)


def solution(mesh):
    return jax.shard_map(
        on_device,
        mesh=mesh,
        in_specs=(
            P(None, None, "gy", "gx"),
            P(None, None, None, "gy", "gx"),
            P("gy", "gx"),
            P(("gy", "gx")),
        ),
        out_specs=(
            P(None, None, "gy", "gx"),
            P(None, "gy", "gx"),
            P(("gy", "gx"), None, None, None),
        ),
        check_vma=False,
    )
```
